32 devices in a mesh: grp: 2 (over x), wide: 16 (over z, y, core).
Axes of the slice: x: 2, y: 2, z: 4, core: 2. Of those that a mesh axis runs over, the one named last changes fastest.
Arguments:
- activations: bfloat16 [128, 2, 32, 4096], P(('grp', 'wide')), parts along dimension 0, may hold values from -6 to 6
- out_grads: bfloat16 [128, 2, 32, 4096], P(('grp', 'wide')), parts along dimension 0, may hold values from -6 to 6
- lengths: int32 [128], P(('grp', 'wide')), parts along dimension 0, may hold values from 1 to 32, as said below
- proj_in: bfloat16 [2, 4096, 128], replicated
- proj_out: bfloat16 [2, 4096, 256], replicated
Outputs:
- precond: bfloat16 [128, 65536], P(('grp', 'wide')), parts along dimension 0
The draws below stay inside these ranges and needn't reach their ends.
There are 2 independent parts, one for each index of `grp`. The reference program is written for one: setup_inputs(seed, part) draws one part's arguments, and reference() takes and returns one part's arrays. A program takes and returns all parts, laid end to end along the dimension named above; an argument that names none is the same for every part. Nothing has to cross between parts.
Inputs may be any that keep to these rules, and one draw needn't show every extreme that they name: `lengths`: some sequence of every group has all 32 tokens valid.
All inputs are finite; a program needn't handle non-finite values.
Results may differ from the reference program's by a relative error of at most 0.0061.
Values may be sent and summed in bfloat16 or wider, within the bound.
A program may use at most 64 MiB of HBM per device.

```python
import math
import jax
import jax.numpy as jnp
from jax import lax

D = 4096
R_OUT = 256
R_IN = 128
NMOD = 2
BLOCK = 512
NS_ITERS = 5
LEN = 32
SEQ_ALL = 64
GD = 65536
BLOCKS = 128


def scaled_columns(key, drawn, shape):
    column_scale = jnp.exp(jax.random.uniform(key, (shape[0], 1, shape[2]), jnp.float32, -0.6931472, 0.6931472))
    return (drawn * column_scale / jnp.sqrt(jnp.float32(D))).astype(jnp.bfloat16)


def draw_proj_in(key, part):
    shape = (NMOD, D, R_IN)
    key_a, key_b = jax.random.split(jax.random.fold_in(key, 11))
    drawn = jax.random.normal(key_a, shape, jnp.float32)
    return scaled_columns(key_b, drawn, shape)


def draw_proj_out(key, part):
    shape = (NMOD, D, R_OUT)
    key_a, key_b = jax.random.split(jax.random.fold_in(key, 23))
    drawn = jax.random.normal(key_a, shape, jnp.float32)
    return scaled_columns(key_b, drawn, shape)


def draw_lengths(key, part):
    key_a, key_b = jax.random.split(jax.random.fold_in(key, 37))
    counts = jax.random.randint(key_a, (SEQ_ALL,), 1, LEN + 1, dtype=jnp.int32)
    chosen = jax.random.randint(key_b, (), 0, SEQ_ALL, dtype=jnp.int32)
    return counts.at[chosen].set(LEN)


def steps_of(stream_key, dims, shards, smallest, high):
    def one(axis_at, parts):
        draws = jax.random.uniform(jax.random.fold_in(jax.random.fold_in(stream_key, 6), axis_at), (parts,), jnp.float32, smallest / len(shards), high / len(shards))
        return jnp.repeat(jnp.exp(draws), dims[axis_at] // parts).reshape((-1,) + (1,) * (len(dims) - axis_at - 1))

    level = one(*shards[0])
    for cut in shards[1:]:
        level = level * one(*cut)
    return level


def centred(rng, shape, width, bound, pieces=(), kind=jnp.bfloat16):
    loudness = steps_of(rng, shape, pieces, -0.22, 0.18) if pieces else 1.0
    values = jax.random.normal(rng, shape, jnp.float32) * width * loudness
    return jnp.minimum(jnp.maximum(values, -bound), bound).astype(kind)


def setup_inputs(seed: int = 0, part: int = 0) -> dict:
    seeds = jax.random.split(jax.random.key(seed), 6)
    own_keys = jax.random.split(jax.random.fold_in(seeds[5], part), 6)
    activations = centred(own_keys[0], (SEQ_ALL, NMOD, LEN, D), 1.0, 6.0, ((0, 16),))
    out_grads = centred(own_keys[1], (SEQ_ALL, NMOD, LEN, D), 1.0, 6.0, ((0, 16),))
    lengths = draw_lengths(jax.random.fold_in(jax.random.fold_in(seeds[5], part), 71), part)
    proj_in = draw_proj_in(jax.random.fold_in(seeds[5], 71), part)
    proj_out = draw_proj_out(jax.random.fold_in(seeds[5], 71), part)
    return {"activations": activations, "out_grads": out_grads, "lengths": lengths, "proj_in": proj_in, "proj_out": proj_out}


def precondition_block(block_rows):
    identity = jnp.eye(BLOCK, dtype=jnp.float32)
    gram_matrix = jnp.dot(block_rows.T, block_rows, precision=lax.Precision.HIGHEST, preferred_element_type=jnp.float32) / SEQ_ALL
    trace_sum = jnp.trace(gram_matrix)
    fisher = gram_matrix + 0.1 * trace_sum / BLOCK * identity
    frobenius = jnp.sqrt(jnp.sum(fisher * fisher))
    inverse = identity / frobenius
    for _ in range(NS_ITERS):
        inverse = jnp.dot(inverse, 2.0 * identity - jnp.dot(fisher, inverse, precision=lax.Precision.HIGHEST), precision=lax.Precision.HIGHEST)
    return jnp.dot(block_rows, inverse, precision=lax.Precision.HIGHEST, preferred_element_type=jnp.float32).astype(jnp.bfloat16)

def reference(activations, out_grads, lengths, proj_in, proj_out):
    positions = jnp.arange(LEN, dtype=jnp.int32)
    valid_mask = (positions[None, :] < lengths[:, None]).astype(jnp.float32)[:, :, None]
    scale_factor = 1.0 / math.sqrt(LEN)
    module_grads = []
    for module in range(NMOD):
        projected_in = jnp.einsum('std,dr->str', activations[:, module].astype(jnp.float32), proj_in[module].astype(jnp.float32))
        projected_in = (projected_in * valid_mask).astype(jnp.bfloat16)
        projected_out = jnp.einsum('std,dr->str', out_grads[:, module].astype(jnp.float32), proj_out[module].astype(jnp.float32))
        projected_out = (projected_out * valid_mask).astype(jnp.bfloat16)
        module_grad = jnp.einsum('sto,sti->soi', projected_out.astype(jnp.float32), projected_in.astype(jnp.float32)) * scale_factor
        module_grads.append(module_grad.reshape(SEQ_ALL, R_OUT * R_IN))
    seq_grads = jnp.concatenate(module_grads, axis=1)
    blocks = seq_grads.reshape(SEQ_ALL, BLOCKS, BLOCK).transpose(1, 0, 2)
    result = lax.map(precondition_block, blocks)
    return result.transpose(1, 0, 2).reshape(SEQ_ALL, GD)
```

```python
import functools
import math

import jax
import jax.numpy as jnp
from jax import lax
from jax.experimental import pallas as pl
from jax.experimental.pallas import tpu as pltpu
from jax.sharding import PartitionSpec as P

BLOCK = 512
NS_ITERS = 5
DAMPING = 0.1
CHUNKS = 2
MESH = pl.DeviceIdType.MESH


def precondition(rows):
    row_count = rows.shape[0]
    order = rows.shape[2]
    highest = lax.Precision.HIGHEST
    identity = jnp.eye(row_count, dtype=jnp.float32)[None]
    gram = jnp.einsum("ska,tka->kst", rows, rows, preferred_element_type=jnp.float32) / row_count
    trace_sum = jnp.trace(gram, axis1=1, axis2=2)[:, None, None]
    damping = DAMPING * trace_sum / order
    squares = jnp.sum(gram * gram, axis=(1, 2), keepdims=True)
    frobenius = jnp.sqrt(squares + 2.0 * damping * trace_sum + order * damping * damping)
    power = identity - (gram + damping * identity) / frobenius
    total = identity + power
    for _ in range(NS_ITERS - 1):
        power = jnp.einsum("kab,kbc->kac", power, power, precision=highest)
        total = total + jnp.einsum("kab,kbc->kac", total, power, precision=highest)
    return jnp.einsum(
        "kst,tka->ska", total / frobenius, rows.astype(jnp.float32), precision=highest
    ).astype(jnp.bfloat16)


def local_plain(activations, out_grads, lengths, proj_in, proj_out):
    seq_count, module_count, seq_len, model_width = activations.shape
    rank_in = proj_in.shape[2]
    rank_out = proj_out.shape[2]
    acc_in = jnp.einsum("smtd,mdr->smtr", activations, proj_in, preferred_element_type=jnp.float32)
    acc_out = jnp.einsum("smtd,mdr->smtr", out_grads, proj_out, preferred_element_type=jnp.float32)
    positions = lax.broadcasted_iota(jnp.int32, (seq_count, seq_len), 1)
    valid_mask = (positions < lengths[:, None]).astype(jnp.float32)[:, None, :, None]
    projected_in = (acc_in * valid_mask).astype(jnp.bfloat16)
    projected_out = (acc_out * valid_mask).astype(jnp.bfloat16)
    seq_grads = jnp.einsum(
        "smto,smti->smoi", projected_out, projected_in, preferred_element_type=jnp.float32
    ) * (1.0 / math.sqrt(seq_len))
    grad_size = module_count * rank_out * rank_in
    wide_count = lax.axis_size("wide")
    blocks_here = grad_size // (BLOCK * wide_count)
    blocks = seq_grads.astype(jnp.bfloat16).reshape(seq_count, wide_count, blocks_here, BLOCK)
    owned_rows = lax.all_to_all(blocks, "wide", split_axis=1, concat_axis=0, tiled=True)
    result = precondition(owned_rows[:, 0])[:, None]
    returned = lax.all_to_all(result, "wide", split_axis=0, concat_axis=1, tiled=True)
    return returned.reshape(seq_count, grad_size)


def split_dot(left, right):
    left_high = left.astype(jnp.bfloat16)
    left_low = (left - left_high.astype(jnp.float32)).astype(jnp.bfloat16)
    right_high = right.astype(jnp.bfloat16)
    right_low = (right - right_high.astype(jnp.float32)).astype(jnp.bfloat16)
    dot = functools.partial(jnp.dot, preferred_element_type=jnp.float32)
    return dot(left_high, right_high) + (dot(left_high, right_low) + dot(left_low, right_high))


def polynomial(stacked, group, order, row_count):
    size = stacked.shape[0]
    row = lax.broadcasted_iota(jnp.int32, (size, size), 0)
    column = lax.broadcasted_iota(jnp.int32, (size, size), 1)
    same = jnp.where(row // row_count == column // row_count, 1.0, 0.0).astype(jnp.float32)
    identity = jnp.where(row == column, 1.0, 0.0).astype(jnp.float32)
    gram = lax.dot_general(
        stacked, stacked, (((1,), (1,)), ((), ())), preferred_element_type=jnp.float32
    )
    gram = jnp.where(row // row_count == column // row_count, gram, 0.0) * (1.0 / row_count)
    diagonal = jnp.sum(gram * identity, axis=0, keepdims=True)
    trace_sum = jnp.sum(same * diagonal, axis=1, keepdims=True)
    squares = jnp.sum(gram * gram, axis=0, keepdims=True)
    squares = jnp.sum(same * squares, axis=1, keepdims=True)
    damping = (DAMPING / order) * trace_sum
    frobenius = jnp.sqrt(squares + 2.0 * damping * trace_sum + order * damping * damping)
    scale = 1.0 / frobenius
    power = identity - (gram + damping * identity) * scale
    total = identity + power
    for _ in range(NS_ITERS - 1):
        power = split_dot(power, power)
        total = total + split_dot(total, power)
    return total * scale


def kernel(
    wide, lengths_ref, act_ref, grad_ref, in_ref, out_proj_ref, result_ref,
    act_v, grad_v, in_v, out_v, outgoing, rows_v, work, finished,
    load_sem, send_sem, recv_sem, back_send_sem, back_recv_sem,
):
    seqs, modules, seq_len, width = act_ref.shape
    rank_in = in_ref.shape[2]
    rank_out = out_proj_ref.shape[2]
    here = rank_out // wide
    all_seqs = seqs * wide
    lanes = BLOCK // rank_in
    blocks = here // lanes
    depth = width // CHUNKS
    me = lax.axis_index("wide")

    def loads(m, c):
        span = pl.ds(c * depth, depth)
        return (
            pltpu.make_async_copy(act_ref.at[:, m, :, span], act_v.at[m, c], load_sem.at[m, c, 0]),
            pltpu.make_async_copy(in_ref.at[m, span, :], in_v.at[m, c], load_sem.at[m, c, 1]),
            pltpu.make_async_copy(grad_ref.at[:, m, :, span], grad_v.at[m, c], load_sem.at[m, c, 2]),
            pltpu.make_async_copy(out_proj_ref.at[m, span, :], out_v.at[m, c], load_sem.at[m, c, 3]),
        )

    for m in range(modules):
        for c in range(CHUNKS):
            for copy in loads(m, c):
                copy.start()

    barrier = pltpu.get_barrier_semaphore()

    def greet(d, carry):
        pl.semaphore_signal(
            barrier, inc=1, device_id={"wide": lax.rem(me + d, wide)}, device_id_type=MESH
        )
        return carry

    lax.fori_loop(1, wide, greet, 0)

    def scatter(m, d):
        target = lax.rem(me + d, wide)
        return pltpu.make_async_remote_copy(
            src_ref=outgoing.at[m, target],
            dst_ref=rows_v.at[m, pl.ds(me * seqs, seqs)],
            send_sem=send_sem.at[m, d],
            recv_sem=recv_sem.at[m, d],
            device_id={"wide": target},
            device_id_type=MESH,
        )

    def give_back(m, d):
        target = lax.rem(me + d, wide)
        return pltpu.make_async_remote_copy(
            src_ref=finished.at[m, pl.ds(target * seqs, seqs)],
            dst_ref=result_ref.at[:, m, pl.ds(pl.multiple_of(me * here, here), here), :],
            send_sem=back_send_sem.at[m, d],
            recv_sem=back_recv_sem.at[m, d],
            device_id={"wide": target},
            device_id_type=MESH,
        )

    def each(action):
        def body(d, carry):
            action(d)
            return carry

        lax.fori_loop(1, wide, body, 0)

    dot = functools.partial(jnp.dot, preferred_element_type=jnp.float32)
    positions = lax.broadcasted_iota(jnp.int32, (seq_len, 1), 0)
    for m in range(modules):
        acc_in = jnp.zeros((seqs * seq_len, rank_in), jnp.float32)
        acc_out = jnp.zeros((seqs * seq_len, rank_out), jnp.float32)
        for c in range(CHUNKS):
            for copy in loads(m, c):
                copy.wait()
            acc_in = acc_in + dot(act_v[m, c].reshape(seqs * seq_len, depth), in_v[m, c])
            acc_out = acc_out + dot(grad_v[m, c].reshape(seqs * seq_len, depth), out_v[m, c])
        for s in range(seqs):
            valid = jnp.where(positions < lengths_ref[s], 1.0, 0.0).astype(jnp.float32)
            part = slice(s * seq_len, (s + 1) * seq_len)
            left = (acc_out[part] * valid).astype(jnp.bfloat16)
            right = (acc_in[part] * valid).astype(jnp.bfloat16)
            product = lax.dot_general(
                left, right, (((0,), (0,)), ((), ())), preferred_element_type=jnp.float32
            ) * (1.0 / math.sqrt(seq_len))
            outgoing[m, :, s] = product.astype(jnp.bfloat16).reshape(wide, here, rank_in)
        if m == 0:
            pl.semaphore_wait(barrier, wide - 1)
        each(lambda d: scatter(m, d).start())
        rows_v[m, pl.ds(me * seqs, seqs)] = outgoing[m, me]

    for m in range(modules):
        each(lambda d: scatter(m, d).wait_recv())
        work[...] = rows_v[m].astype(jnp.float32).reshape(all_seqs * here, rank_in)
        stacked = jnp.concatenate(
            [
                jnp.concatenate(
                    [
                        work[pl.ds(b * lanes + j, all_seqs, stride=here), :].astype(jnp.bfloat16)
                        for j in range(lanes)
                    ],
                    axis=1,
                )
                for b in range(blocks)
            ],
            axis=0,
        )
        inverse = polynomial(stacked, blocks, BLOCK, all_seqs)
        high = inverse.astype(jnp.bfloat16)
        low = (inverse - high.astype(jnp.float32)).astype(jnp.bfloat16)
        solved = dot(high, stacked) + dot(low, stacked)
        for b in range(blocks):
            for j in range(lanes):
                work[pl.ds(b * lanes + j, all_seqs, stride=here), :] = solved[
                    b * all_seqs : (b + 1) * all_seqs, j * rank_in : (j + 1) * rank_in
                ]
        finished[m] = work[...].astype(jnp.bfloat16).reshape(all_seqs, here, rank_in)
        each(lambda d: give_back(m, d).start())
        result_ref[:, m, pl.ds(pl.multiple_of(me * here, here), here), :] = finished[
            m, pl.ds(me * seqs, seqs)
        ]

    for m in range(modules):
        each(lambda d: scatter(m, d).wait_send())
        each(lambda d: give_back(m, d).wait_recv())
        each(lambda d: give_back(m, d).wait_send())


def local_fused(wide, activations, out_grads, lengths, proj_in, proj_out):
    seqs, modules, seq_len, width = activations.shape
    rank_in = proj_in.shape[2]
    rank_out = proj_out.shape[2]
    here = rank_out // wide
    depth = width // CHUNKS
    all_seqs = seqs * wide
    any_spec = pl.BlockSpec(memory_space=pl.ANY)
    bf16 = jnp.bfloat16
    out = pl.pallas_call(
        functools.partial(kernel, wide),
        out_shape=jax.ShapeDtypeStruct((seqs, modules, rank_out, rank_in), bf16),
        in_specs=[pl.BlockSpec(memory_space=pltpu.SMEM)] + [any_spec] * 4,
        out_specs=pl.BlockSpec(memory_space=pltpu.VMEM),
        scratch_shapes=[
            pltpu.VMEM((modules, CHUNKS, seqs, seq_len, depth), bf16),
            pltpu.VMEM((modules, CHUNKS, seqs, seq_len, depth), bf16),
            pltpu.VMEM((modules, CHUNKS, depth, rank_in), bf16),
            pltpu.VMEM((modules, CHUNKS, depth, rank_out), bf16),
            pltpu.VMEM((modules, wide, seqs, here, rank_in), bf16),
            pltpu.VMEM((modules, all_seqs, here, rank_in), bf16),
            pltpu.VMEM((all_seqs * here, rank_in), jnp.float32),
            pltpu.VMEM((modules, all_seqs, here, rank_in), bf16),
            pltpu.SemaphoreType.DMA((modules, CHUNKS, 4)),
            pltpu.SemaphoreType.DMA((modules, wide)),
            pltpu.SemaphoreType.DMA((modules, wide)),
            pltpu.SemaphoreType.DMA((modules, wide)),
            pltpu.SemaphoreType.DMA((modules, wide)),
        ],
        compiler_params=pltpu.CompilerParams(
            collective_id=0, has_side_effects=True, vmem_limit_bytes=40 * 1024 * 1024
        ),
    )(lengths, activations, out_grads, proj_in, proj_out)
    return out.reshape(seqs, modules * rank_out * rank_in)


def solution(mesh):
    in_specs = (
        P(("grp", "wide"), None, None, None),
        P(("grp", "wide"), None, None, None),
        P(("grp", "wide")),
        P(),
        P(),
    )
    out_specs = P(("grp", "wide"), None)
    wide = mesh.shape["wide"]

    def local(activations, out_grads, lengths, proj_in, proj_out):
        here = proj_out.shape[2] // wide
        lanes = BLOCK // proj_in.shape[2]
        stacked = activations.shape[0] * wide * max(here // lanes, 1)
        if here % 16 == 0 and here % lanes == 0 and stacked <= 512:
            return local_fused(wide, activations, out_grads, lengths, proj_in, proj_out)
        return local_plain(activations, out_grads, lengths, proj_in, proj_out)

    return jax.shard_map(
        local, mesh=mesh, in_specs=in_specs, out_specs=out_specs, check_vma=False
    )
```

```python
import functools
import math

import jax
import jax.numpy as jnp
from jax import lax
from jax.experimental import pallas as pl
from jax.experimental.pallas import tpu as pltpu
from jax.sharding import PartitionSpec as P

BLOCK = 512
NS_ITERS = 5
DAMPING = 0.1
CHUNKS = 2
MESH = pl.DeviceIdType.MESH


def precondition(rows):
    row_count = rows.shape[0]
    order = rows.shape[2]
    highest = lax.Precision.HIGHEST
    identity = jnp.eye(row_count, dtype=jnp.float32)[None]
    gram = jnp.einsum("ska,tka->kst", rows, rows, preferred_element_type=jnp.float32) / row_count
    trace_sum = jnp.trace(gram, axis1=1, axis2=2)[:, None, None]
    damping = DAMPING * trace_sum / order
    squares = jnp.sum(gram * gram, axis=(1, 2), keepdims=True)
    frobenius = jnp.sqrt(squares + 2.0 * damping * trace_sum + order * damping * damping)
    power = identity - (gram + damping * identity) / frobenius
    total = identity + power
    for _ in range(NS_ITERS - 1):
        power = jnp.einsum("kab,kbc->kac", power, power, precision=highest)
        total = total + jnp.einsum("kab,kbc->kac", total, power, precision=highest)
    return jnp.einsum(
        "kst,tka->ska", total / frobenius, rows.astype(jnp.float32), precision=highest
    ).astype(jnp.bfloat16)


def local_plain(activations, out_grads, lengths, proj_in, proj_out):
    seq_count, module_count, seq_len, model_width = activations.shape
    rank_in = proj_in.shape[2]
    rank_out = proj_out.shape[2]
    acc_in = jnp.einsum("smtd,mdr->smtr", activations, proj_in, preferred_element_type=jnp.float32)
    acc_out = jnp.einsum("smtd,mdr->smtr", out_grads, proj_out, preferred_element_type=jnp.float32)
    positions = lax.broadcasted_iota(jnp.int32, (seq_count, seq_len), 1)
    valid_mask = (positions < lengths[:, None]).astype(jnp.float32)[:, None, :, None]
    projected_in = (acc_in * valid_mask).astype(jnp.bfloat16)
    projected_out = (acc_out * valid_mask).astype(jnp.bfloat16)
    seq_grads = jnp.einsum(
        "smto,smti->smoi", projected_out, projected_in, preferred_element_type=jnp.float32
    ) * (1.0 / math.sqrt(seq_len))
    grad_size = module_count * rank_out * rank_in
    wide_count = lax.axis_size("wide")
    blocks_here = grad_size // (BLOCK * wide_count)
    blocks = seq_grads.astype(jnp.bfloat16).reshape(seq_count, wide_count, blocks_here, BLOCK)
    owned_rows = lax.all_to_all(blocks, "wide", split_axis=1, concat_axis=0, tiled=True)
    result = precondition(owned_rows[:, 0])[:, None]
    returned = lax.all_to_all(result, "wide", split_axis=0, concat_axis=1, tiled=True)
    return returned.reshape(seq_count, grad_size)


def polynomial(stacked, order, row_count):
    size = stacked.shape[0]
    blocks = size // row_count
    row = lax.broadcasted_iota(jnp.int32, (size, size), 0)
    column = lax.broadcasted_iota(jnp.int32, (size, size), 1)
    same = row // row_count == column // row_count
    short = (row_count, size)
    lane = lax.broadcasted_iota(jnp.int32, (1, size), 1)
    on_diagonal = (
        lax.broadcasted_iota(jnp.int32, short, 0)
        == lax.broadcasted_iota(jnp.int32, short, 1) % row_count
    )
    identity = jnp.where(on_diagonal, 1.0, 0.0).astype(jnp.float32)

    def spread(beside):
        tall = jnp.concatenate([beside] * blocks, axis=0)
        return jnp.where(same, tall, 0.0).astype(jnp.bfloat16)

    def halves(beside):
        high = beside.astype(jnp.bfloat16).astype(jnp.float32)
        return high, beside - high

    def per_block(values):
        total = jnp.zeros((1, size), jnp.float32)
        for b in range(blocks):
            mine = lane // row_count == b
            part = jnp.sum(jnp.where(mine, values, 0.0), axis=1, keepdims=True)
            total = jnp.where(mine, part, total)
        return total

    dot = functools.partial(jnp.dot, preferred_element_type=jnp.float32)
    gram = lax.dot_general(
        stacked, stacked, (((1,), (1,)), ((), ())), preferred_element_type=jnp.float32
    )
    gram = jnp.where(same, gram, 0.0)
    beside = gram[:row_count]
    for b in range(1, blocks):
        beside = beside + gram[b * row_count : (b + 1) * row_count]
    beside = beside * (1.0 / row_count)
    trace_sum = per_block(jnp.sum(beside * identity, axis=0, keepdims=True))
    squares = per_block(jnp.sum(beside * beside, axis=0, keepdims=True))
    damping = (DAMPING / order) * trace_sum
    frobenius = jnp.sqrt(squares + 2.0 * damping * trace_sum + order * damping * damping)
    scale = 1.0 / frobenius
    power = identity - (beside + damping * identity) * scale
    total = identity + power
    for step in range(NS_ITERS):
        high, low = halves(power)
        right_high, right_low = spread(high), spread(low)
        if step == 0:
            left_high, left_low = high.astype(jnp.bfloat16), low.astype(jnp.bfloat16)
        elif step < NS_ITERS - 1:
            total_high, total_low = halves(total)
            left_high = jnp.concatenate([total_high, high], axis=0).astype(jnp.bfloat16)
            left_low = jnp.concatenate([total_low, low], axis=0).astype(jnp.bfloat16)
        else:
            total_high, total_low = halves(total)
            left_high, left_low = total_high.astype(jnp.bfloat16), total_low.astype(jnp.bfloat16)
        product = dot(left_high, right_high) + (
            dot(left_high, right_low) + dot(left_low, right_high)
        )
        if step == 0:
            power = product
        else:
            total = total + product[:row_count]
            power = product[row_count:]
    high, low = halves(total * scale)
    return spread(high), spread(low)


def kernel(
    wide, lengths_ref, act_ref, grad_ref, in_ref, out_proj_ref, result_ref,
    act_v, grad_v, in_v, out_v, outgoing, rows_v, work, finished,
    load_sem, send_sem, recv_sem, back_send_sem, back_recv_sem,
):
    seqs, modules, seq_len, width = act_ref.shape
    rank_in = in_ref.shape[2]
    rank_out = out_proj_ref.shape[2]
    here = rank_out // wide
    all_seqs = seqs * wide
    lanes = BLOCK // rank_in
    blocks = here // lanes
    depth = width // CHUNKS
    me = lax.axis_index("wide")

    def loads(m, c):
        span = pl.ds(c * depth, depth)
        return (
            pltpu.make_async_copy(act_ref.at[:, m, :, span], act_v.at[m, c], load_sem.at[m, c, 0]),
            pltpu.make_async_copy(in_ref.at[m, span, :], in_v.at[m, c], load_sem.at[m, c, 1]),
            pltpu.make_async_copy(grad_ref.at[:, m, :, span], grad_v.at[m, c], load_sem.at[m, c, 2]),
            pltpu.make_async_copy(out_proj_ref.at[m, span, :], out_v.at[m, c], load_sem.at[m, c, 3]),
        )

    for c in range(CHUNKS):
        for copy in loads(0, c):
            copy.start()

    barrier = pltpu.get_barrier_semaphore()

    def greet(d, carry):
        pl.semaphore_signal(
            barrier, inc=1, device_id={"wide": lax.rem(me + d, wide)}, device_id_type=MESH
        )
        return carry

    lax.fori_loop(1, wide, greet, 0)

    def scatter(m, d):
        target = lax.rem(me + d, wide)
        return pltpu.make_async_remote_copy(
            src_ref=outgoing.at[m, target],
            dst_ref=rows_v.at[m, pl.ds(me * seqs, seqs)],
            send_sem=send_sem.at[m, d],
            recv_sem=recv_sem.at[m, d],
            device_id={"wide": target},
            device_id_type=MESH,
        )

    def give_back(m, d):
        target = lax.rem(me + d, wide)
        return pltpu.make_async_remote_copy(
            src_ref=finished.at[m, pl.ds(target * seqs, seqs)],
            dst_ref=result_ref.at[:, m, pl.ds(pl.multiple_of(me * here, here), here), :],
            send_sem=back_send_sem.at[m, d],
            recv_sem=back_recv_sem.at[m, d],
            device_id={"wide": target},
            device_id_type=MESH,
        )

    def each(action):
        def body(i, carry):
            action(wide // 2 + (2 * (i % 2) - 1) * ((i + 1) // 2))
            return carry

        lax.fori_loop(0, wide - 1, body, 0)

    dot = functools.partial(jnp.dot, preferred_element_type=jnp.float32)
    positions = lax.broadcasted_iota(jnp.int32, (seq_len, 1), 0)
    for m in range(modules):
        acc_in = jnp.zeros((seqs * seq_len, rank_in), jnp.float32)
        acc_out = jnp.zeros((seqs * seq_len, rank_out), jnp.float32)
        for c in range(CHUNKS):
            for copy in loads(m, c):
                copy.wait()
            if m + 1 < modules:
                for copy in loads(m + 1, c):
                    copy.start()
            acc_in = acc_in + dot(act_v[m, c].reshape(seqs * seq_len, depth), in_v[m, c])
            acc_out = acc_out + dot(grad_v[m, c].reshape(seqs * seq_len, depth), out_v[m, c])
        for s in range(seqs):
            valid = jnp.where(positions < lengths_ref[s], 1.0, 0.0).astype(jnp.float32)
            part = slice(s * seq_len, (s + 1) * seq_len)
            left = (acc_out[part] * valid).astype(jnp.bfloat16)
            right = (acc_in[part] * valid).astype(jnp.bfloat16)
            product = lax.dot_general(
                left, right, (((0,), (0,)), ((), ())), preferred_element_type=jnp.float32
            ) * (1.0 / math.sqrt(seq_len))
            outgoing[m, :, s] = product.astype(jnp.bfloat16).reshape(wide, here, rank_in)
        if m == 0:
            pl.semaphore_wait(barrier, wide - 1)
        each(lambda d: scatter(m, d).start())
        rows_v[m, pl.ds(me * seqs, seqs)] = outgoing[m, me]

    for m in range(modules):
        each(lambda d: scatter(m, d).wait_recv())
        work[...] = rows_v[m].astype(jnp.float32).reshape(all_seqs * here, rank_in)
        stacked = jnp.concatenate(
            [
                jnp.concatenate(
                    [
                        work[pl.ds(b * lanes + j, all_seqs, stride=here), :].astype(jnp.bfloat16)
                        for j in range(lanes)
                    ],
                    axis=1,
                )
                for b in range(blocks)
            ],
            axis=0,
        )
        high, low = polynomial(stacked, BLOCK, all_seqs)
        solved = dot(high, stacked) + dot(low, stacked)
        for b in range(blocks):
            for j in range(lanes):
                work[pl.ds(b * lanes + j, all_seqs, stride=here), :] = solved[
                    b * all_seqs : (b + 1) * all_seqs, j * rank_in : (j + 1) * rank_in
                ]
        finished[m] = work[...].astype(jnp.bfloat16).reshape(all_seqs, here, rank_in)
        each(lambda d: give_back(m, d).start())
        result_ref[:, m, pl.ds(pl.multiple_of(me * here, here), here), :] = finished[
            m, pl.ds(me * seqs, seqs)
        ]

    for m in range(modules):
        each(lambda d: scatter(m, d).wait_send())
        each(lambda d: give_back(m, d).wait_recv())
        each(lambda d: give_back(m, d).wait_send())


def local_fused(wide, activations, out_grads, lengths, proj_in, proj_out):
    seqs, modules, seq_len, width = activations.shape
    rank_in = proj_in.shape[2]
    rank_out = proj_out.shape[2]
    here = rank_out // wide
    depth = width // CHUNKS
    all_seqs = seqs * wide
    any_spec = pl.BlockSpec(memory_space=pl.ANY)
    bf16 = jnp.bfloat16
    out = pl.pallas_call(
        functools.partial(kernel, wide),
        out_shape=jax.ShapeDtypeStruct((seqs, modules, rank_out, rank_in), bf16),
        in_specs=[pl.BlockSpec(memory_space=pltpu.SMEM)] + [any_spec] * 4,
        out_specs=pl.BlockSpec(memory_space=pltpu.VMEM),
        scratch_shapes=[
            pltpu.VMEM((modules, CHUNKS, seqs, seq_len, depth), bf16),
            pltpu.VMEM((modules, CHUNKS, seqs, seq_len, depth), bf16),
            pltpu.VMEM((modules, CHUNKS, depth, rank_in), bf16),
            pltpu.VMEM((modules, CHUNKS, depth, rank_out), bf16),
            pltpu.VMEM((modules, wide, seqs, here, rank_in), bf16),
            pltpu.VMEM((modules, all_seqs, here, rank_in), bf16),
            pltpu.VMEM((all_seqs * here, rank_in), jnp.float32),
            pltpu.VMEM((modules, all_seqs, here, rank_in), bf16),
            pltpu.SemaphoreType.DMA((modules, CHUNKS, 4)),
            pltpu.SemaphoreType.DMA((modules, wide)),
            pltpu.SemaphoreType.DMA((modules, wide)),
            pltpu.SemaphoreType.DMA((modules, wide)),
            pltpu.SemaphoreType.DMA((modules, wide)),
        ],
        compiler_params=pltpu.CompilerParams(
            collective_id=0, has_side_effects=True, vmem_limit_bytes=60 * 1024 * 1024
        ),
    )(lengths, activations, out_grads, proj_in, proj_out)
    return out.reshape(seqs, modules * rank_out * rank_in)


def solution(mesh):
    in_specs = (
        P(("grp", "wide"), None, None, None),
        P(("grp", "wide"), None, None, None),
        P(("grp", "wide")),
        P(),
        P(),
    )
    out_specs = P(("grp", "wide"), None)
    wide = mesh.shape["wide"]

    def local(activations, out_grads, lengths, proj_in, proj_out):
        here = proj_out.shape[2] // wide
        lanes = BLOCK // proj_in.shape[2]
        stacked = activations.shape[0] * wide * max(here // lanes, 1)
        if here % 16 == 0 and here % lanes == 0 and stacked <= 512:
            return local_fused(wide, activations, out_grads, lengths, proj_in, proj_out)
        return local_plain(activations, out_grads, lengths, proj_in, proj_out)

    return jax.shard_map(
        local, mesh=mesh, in_specs=in_specs, out_specs=out_specs, check_vma=False
    )
```

```python
import functools
import math

import jax
import jax.numpy as jnp
from jax import lax
from jax.experimental import pallas as pl
from jax.experimental.pallas import tpu as pltpu
from jax.sharding import PartitionSpec as P

BLOCK = 512
NS_ITERS = 5
DAMPING = 0.1
CHUNKS = 4
MESH = pl.DeviceIdType.MESH


def precondition(rows):
    row_count = rows.shape[0]
    order = rows.shape[2]
    highest = lax.Precision.HIGHEST
    identity = jnp.eye(row_count, dtype=jnp.float32)[None]
    gram = jnp.einsum("ska,tka->kst", rows, rows, preferred_element_type=jnp.float32) / row_count
    trace_sum = jnp.trace(gram, axis1=1, axis2=2)[:, None, None]
    damping = DAMPING * trace_sum / order
    squares = jnp.sum(gram * gram, axis=(1, 2), keepdims=True)
    frobenius = jnp.sqrt(squares + 2.0 * damping * trace_sum + order * damping * damping)
    power = identity - (gram + damping * identity) / frobenius
    total = identity + power
    for _ in range(NS_ITERS - 1):
        power = jnp.einsum("kab,kbc->kac", power, power, precision=highest)
        total = total + jnp.einsum("kab,kbc->kac", total, power, precision=highest)
    return jnp.einsum(
        "kst,tka->ska", total / frobenius, rows.astype(jnp.float32), precision=highest
    ).astype(jnp.bfloat16)


def local_plain(activations, out_grads, lengths, proj_in, proj_out):
    seq_count, module_count, seq_len, model_width = activations.shape
    rank_in = proj_in.shape[2]
    rank_out = proj_out.shape[2]
    acc_in = jnp.einsum("smtd,mdr->smtr", activations, proj_in, preferred_element_type=jnp.float32)
    acc_out = jnp.einsum("smtd,mdr->smtr", out_grads, proj_out, preferred_element_type=jnp.float32)
    positions = lax.broadcasted_iota(jnp.int32, (seq_count, seq_len), 1)
    valid_mask = (positions < lengths[:, None]).astype(jnp.float32)[:, None, :, None]
    projected_in = (acc_in * valid_mask).astype(jnp.bfloat16)
    projected_out = (acc_out * valid_mask).astype(jnp.bfloat16)
    seq_grads = jnp.einsum(
        "smto,smti->smoi", projected_out, projected_in, preferred_element_type=jnp.float32
    ) * (1.0 / math.sqrt(seq_len))
    grad_size = module_count * rank_out * rank_in
    wide_count = lax.axis_size("wide")
    blocks_here = grad_size // (BLOCK * wide_count)
    blocks = seq_grads.astype(jnp.bfloat16).reshape(seq_count, wide_count, blocks_here, BLOCK)
    owned_rows = lax.all_to_all(blocks, "wide", split_axis=1, concat_axis=0, tiled=True)
    result = precondition(owned_rows[:, 0])[:, None]
    returned = lax.all_to_all(result, "wide", split_axis=0, concat_axis=1, tiled=True)
    return returned.reshape(seq_count, grad_size)


def polynomial(stacked, order, row_count):
    size = stacked.shape[0]
    blocks = size // row_count
    row = lax.broadcasted_iota(jnp.int32, (size, size), 0)
    column = lax.broadcasted_iota(jnp.int32, (size, size), 1)
    same = row // row_count == column // row_count
    short = (row_count, size)
    lane = lax.broadcasted_iota(jnp.int32, (1, size), 1)
    on_diagonal = (
        lax.broadcasted_iota(jnp.int32, short, 0)
        == lax.broadcasted_iota(jnp.int32, short, 1) % row_count
    )
    identity = jnp.where(on_diagonal, 1.0, 0.0).astype(jnp.float32)

    def spread(beside):
        tall = jnp.concatenate([beside] * blocks, axis=0)
        return jnp.where(same, tall, 0.0).astype(jnp.bfloat16)

    def halves(beside):
        high = beside.astype(jnp.bfloat16).astype(jnp.float32)
        return high, beside - high

    def per_block(values):
        total = jnp.zeros((1, size), jnp.float32)
        for b in range(blocks):
            mine = lane // row_count == b
            part = jnp.sum(jnp.where(mine, values, 0.0), axis=1, keepdims=True)
            total = jnp.where(mine, part, total)
        return total

    dot = functools.partial(jnp.dot, preferred_element_type=jnp.float32)
    gram = lax.dot_general(
        stacked, stacked, (((1,), (1,)), ((), ())), preferred_element_type=jnp.float32
    )
    gram = jnp.where(same, gram, 0.0)
    beside = gram[:row_count]
    for b in range(1, blocks):
        beside = beside + gram[b * row_count : (b + 1) * row_count]
    beside = beside * (1.0 / row_count)
    trace_sum = per_block(jnp.sum(beside * identity, axis=0, keepdims=True))
    squares = per_block(jnp.sum(beside * beside, axis=0, keepdims=True))
    damping = (DAMPING / order) * trace_sum
    frobenius = jnp.sqrt(squares + 2.0 * damping * trace_sum + order * damping * damping)
    scale = 1.0 / frobenius
    power = identity - (beside + damping * identity) * scale
    total = identity + power
    for step in range(NS_ITERS):
        high, low = halves(power)
        right_high, right_low = spread(high), spread(low)
        if step == 0:
            left_high, left_low = high.astype(jnp.bfloat16), low.astype(jnp.bfloat16)
        elif step < NS_ITERS - 1:
            total_high, total_low = halves(total)
            left_high = jnp.concatenate([total_high, high], axis=0).astype(jnp.bfloat16)
            left_low = jnp.concatenate([total_low, low], axis=0).astype(jnp.bfloat16)
        else:
            total_high, total_low = halves(total)
            left_high, left_low = total_high.astype(jnp.bfloat16), total_low.astype(jnp.bfloat16)
        product = dot(left_high, right_high) + (
            dot(left_high, right_low) + dot(left_low, right_high)
        )
        if step == 0:
            power = product
        else:
            total = total + product[:row_count]
            power = product[row_count:]
    high, low = halves(total * scale)
    return spread(high), spread(low)


def kernel(
    wide, lengths_ref, act_ref, grad_ref, in_ref, out_proj_ref, result_ref,
    act_v, grad_v, in_v, out_v, outgoing, rows_v, work, finished, returned,
    load_sem, send_sem, recv_sem, back_send_sem, back_recv_sem,
):
    seqs, modules, seq_len, width = act_ref.shape
    rank_in = in_ref.shape[2]
    rank_out = out_proj_ref.shape[2]
    here = rank_out // wide
    all_seqs = seqs * wide
    lanes = BLOCK // rank_in
    blocks = here // lanes
    depth = width // CHUNKS
    me = lax.axis_index("wide")

    def loads(m, c):
        span = pl.ds(c * depth, depth)
        return (
            pltpu.make_async_copy(act_ref.at[:, m, :, span], act_v.at[m, c], load_sem.at[m, c, 0]),
            pltpu.make_async_copy(in_ref.at[m, span, :], in_v.at[m, c], load_sem.at[m, c, 1]),
            pltpu.make_async_copy(grad_ref.at[:, m, :, span], grad_v.at[m, c], load_sem.at[m, c, 2]),
            pltpu.make_async_copy(out_proj_ref.at[m, span, :], out_v.at[m, c], load_sem.at[m, c, 3]),
        )

    for c in range(CHUNKS):
        for copy in loads(0, c):
            copy.start()

    barrier = pltpu.get_barrier_semaphore()

    def greet(d, carry):
        pl.semaphore_signal(
            barrier, inc=1, device_id={"wide": lax.rem(me + d, wide)}, device_id_type=MESH
        )
        return carry

    lax.fori_loop(1, wide, greet, 0)

    def scatter(m, d):
        target = lax.rem(me + d, wide)
        return pltpu.make_async_remote_copy(
            src_ref=outgoing.at[m, target],
            dst_ref=rows_v.at[m, pl.ds(me * seqs, seqs)],
            send_sem=send_sem.at[m, d],
            recv_sem=recv_sem.at[m, d],
            device_id={"wide": target},
            device_id_type=MESH,
        )

    def give_back(m, d):
        target = lax.rem(me + d, wide)
        return pltpu.make_async_remote_copy(
            src_ref=finished.at[m, pl.ds(target * seqs, seqs)],
            dst_ref=returned.at[m, me],
            send_sem=back_send_sem.at[m, d],
            recv_sem=back_recv_sem.at[m, d],
            device_id={"wide": target},
            device_id_type=MESH,
        )

    def each(action):
        def body(i, carry):
            action(wide // 2 + (2 * (i % 2) - 1) * ((i + 1) // 2))
            return carry

        lax.fori_loop(0, wide - 1, body, 0, unroll=5)

    dot = functools.partial(jnp.dot, preferred_element_type=jnp.float32)
    positions = lax.broadcasted_iota(jnp.int32, (seq_len, 1), 0)
    for m in range(modules):
        acc_in = jnp.zeros((seqs * seq_len, rank_in), jnp.float32)
        acc_out = jnp.zeros((seqs * seq_len, rank_out), jnp.float32)
        for c in range(CHUNKS):
            for copy in loads(m, c):
                copy.wait()
            if m + 1 < modules:
                for copy in loads(m + 1, c):
                    copy.start()
            acc_in = acc_in + dot(act_v[m, c].reshape(seqs * seq_len, depth), in_v[m, c])
            acc_out = acc_out + dot(grad_v[m, c].reshape(seqs * seq_len, depth), out_v[m, c])
        for s in range(seqs):
            valid = jnp.where(positions < lengths_ref[s], 1.0, 0.0).astype(jnp.float32)
            part = slice(s * seq_len, (s + 1) * seq_len)
            left = (acc_out[part] * valid).astype(jnp.bfloat16)
            right = (acc_in[part] * valid).astype(jnp.bfloat16)
            product = lax.dot_general(
                left, right, (((0,), (0,)), ((), ())), preferred_element_type=jnp.float32
            ) * (1.0 / math.sqrt(seq_len))
            outgoing[m, :, s] = product.astype(jnp.bfloat16).reshape(wide, here, rank_in)
        if m == 0:
            pl.semaphore_wait(barrier, wide - 1)
        each(lambda d: scatter(m, d).start())
        rows_v[m, pl.ds(me * seqs, seqs)] = outgoing[m, me]

    for m in range(modules):
        each(lambda d: scatter(m, d).wait_recv())
        work[...] = rows_v[m].astype(jnp.float32).reshape(all_seqs * here, rank_in)
        stacked = jnp.concatenate(
            [
                jnp.concatenate(
                    [
                        work[pl.ds(b * lanes + j, all_seqs, stride=here), :].astype(jnp.bfloat16)
                        for j in range(lanes)
                    ],
                    axis=1,
                )
                for b in range(blocks)
            ],
            axis=0,
        )
        high, low = polynomial(stacked, BLOCK, all_seqs)
        solved = dot(high, stacked) + dot(low, stacked)
        for b in range(blocks):
            for j in range(lanes):
                work[pl.ds(b * lanes + j, all_seqs, stride=here), :] = solved[
                    b * all_seqs : (b + 1) * all_seqs, j * rank_in : (j + 1) * rank_in
                ]
        finished[m] = work[...].astype(jnp.bfloat16).reshape(all_seqs, here, rank_in)
        each(lambda d: give_back(m, d).start())
        returned[m, me] = finished[m, pl.ds(me * seqs, seqs)]

    for m in range(modules):
        each(lambda d: scatter(m, d).wait_send())
        each(lambda d: give_back(m, d).wait_recv())
        work[...] = returned[m].astype(jnp.float32).reshape(all_seqs * here, rank_in)

        def place(w, carry):
            for o in range(here):
                start = w * (seqs * here) + o
                lane = pl.multiple_of(((m * wide + w) * here + o) * rank_in, rank_in)
                result_ref[:, pl.ds(lane, rank_in)] = work[
                    pl.ds(start, seqs, stride=here), :
                ].astype(jnp.bfloat16)
            return carry

        lax.fori_loop(0, wide, place, 0)
    for m in range(modules):
        each(lambda d: give_back(m, d).wait_send())


def local_fused(wide, activations, out_grads, lengths, proj_in, proj_out):
    seqs, modules, seq_len, width = activations.shape
    rank_in = proj_in.shape[2]
    rank_out = proj_out.shape[2]
    here = rank_out // wide
    depth = width // CHUNKS
    all_seqs = seqs * wide
    any_spec = pl.BlockSpec(memory_space=pl.ANY)
    bf16 = jnp.bfloat16
    return pl.pallas_call(
        functools.partial(kernel, wide),
        out_shape=jax.ShapeDtypeStruct((seqs, modules * rank_out * rank_in), bf16),
        in_specs=[pl.BlockSpec(memory_space=pltpu.SMEM)] + [any_spec] * 4,
        out_specs=pl.BlockSpec(memory_space=pltpu.VMEM),
        scratch_shapes=[
            pltpu.VMEM((modules, CHUNKS, seqs, seq_len, depth), bf16),
            pltpu.VMEM((modules, CHUNKS, seqs, seq_len, depth), bf16),
            pltpu.VMEM((modules, CHUNKS, depth, rank_in), bf16),
            pltpu.VMEM((modules, CHUNKS, depth, rank_out), bf16),
            pltpu.VMEM((modules, wide, seqs, here, rank_in), bf16),
            pltpu.VMEM((modules, all_seqs, here, rank_in), bf16),
            pltpu.VMEM((all_seqs * here, rank_in), jnp.float32),
            pltpu.VMEM((modules, all_seqs, here, rank_in), bf16),
            pltpu.VMEM((modules, wide, seqs, here, rank_in), bf16),
            pltpu.SemaphoreType.DMA((modules, CHUNKS, 4)),
            pltpu.SemaphoreType.DMA((modules, wide)),
            pltpu.SemaphoreType.DMA((modules, wide)),
            pltpu.SemaphoreType.DMA((modules, wide)),
            pltpu.SemaphoreType.DMA((modules, wide)),
        ],
        compiler_params=pltpu.CompilerParams(
            collective_id=0, has_side_effects=True, vmem_limit_bytes=58 * 1024 * 1024
        ),
    )(lengths, activations, out_grads, proj_in, proj_out)


def solution(mesh):
    in_specs = (
        P(("grp", "wide"), None, None, None),
        P(("grp", "wide"), None, None, None),
        P(("grp", "wide")),
        P(),
        P(),
    )
    out_specs = P(("grp", "wide"), None)
    wide = mesh.shape["wide"]

    def local(activations, out_grads, lengths, proj_in, proj_out):
        here = proj_out.shape[2] // wide
        lanes = BLOCK // proj_in.shape[2]
        stacked = activations.shape[0] * wide * max(here // lanes, 1)
        if here % 16 == 0 and here % lanes == 0 and stacked <= 512:
            return local_fused(wide, activations, out_grads, lengths, proj_in, proj_out)
        return local_plain(activations, out_grads, lengths, proj_in, proj_out)

    return jax.shard_map(
        local, mesh=mesh, in_specs=in_specs, out_specs=out_specs, check_vma=False
    )
```

```python
import functools
import math

import jax
import jax.numpy as jnp
from jax import lax
from jax.experimental import pallas as pl
from jax.experimental.pallas import tpu as pltpu
from jax.sharding import PartitionSpec as P

BLOCK = 512
NS_ITERS = 5
DAMPING = 0.1
CHUNKS = 4
MESH = pl.DeviceIdType.MESH


def precondition(rows):
    row_count = rows.shape[0]
    order = rows.shape[2]
    highest = lax.Precision.HIGHEST
    identity = jnp.eye(row_count, dtype=jnp.float32)[None]
    gram = jnp.einsum("ska,tka->kst", rows, rows, preferred_element_type=jnp.float32) / row_count
    trace_sum = jnp.trace(gram, axis1=1, axis2=2)[:, None, None]
    damping = DAMPING * trace_sum / order
    squares = jnp.sum(gram * gram, axis=(1, 2), keepdims=True)
    frobenius = jnp.sqrt(squares + 2.0 * damping * trace_sum + order * damping * damping)
    power = identity - (gram + damping * identity) / frobenius
    total = identity + power
    for _ in range(NS_ITERS - 1):
        power = jnp.einsum("kab,kbc->kac", power, power, precision=highest)
        total = total + jnp.einsum("kab,kbc->kac", total, power, precision=highest)
    return jnp.einsum(
        "kst,tka->ska", total / frobenius, rows.astype(jnp.float32), precision=highest
    ).astype(jnp.bfloat16)


def local_plain(activations, out_grads, lengths, proj_in, proj_out):
    seq_count, module_count, seq_len, model_width = activations.shape
    rank_in = proj_in.shape[2]
    rank_out = proj_out.shape[2]
    acc_in = jnp.einsum("smtd,mdr->smtr", activations, proj_in, preferred_element_type=jnp.float32)
    acc_out = jnp.einsum("smtd,mdr->smtr", out_grads, proj_out, preferred_element_type=jnp.float32)
    positions = lax.broadcasted_iota(jnp.int32, (seq_count, seq_len), 1)
    valid_mask = (positions < lengths[:, None]).astype(jnp.float32)[:, None, :, None]
    projected_in = (acc_in * valid_mask).astype(jnp.bfloat16)
    projected_out = (acc_out * valid_mask).astype(jnp.bfloat16)
    seq_grads = jnp.einsum(
        "smto,smti->smoi", projected_out, projected_in, preferred_element_type=jnp.float32
    ) * (1.0 / math.sqrt(seq_len))
    grad_size = module_count * rank_out * rank_in
    wide_count = lax.axis_size("wide")
    blocks_here = grad_size // (BLOCK * wide_count)
    blocks = seq_grads.astype(jnp.bfloat16).reshape(seq_count, wide_count, blocks_here, BLOCK)
    owned_rows = lax.all_to_all(blocks, "wide", split_axis=1, concat_axis=0, tiled=True)
    result = precondition(owned_rows[:, 0])[:, None]
    returned = lax.all_to_all(result, "wide", split_axis=0, concat_axis=1, tiled=True)
    return returned.reshape(seq_count, grad_size)


def polynomial(stacked, order, row_count):
    size = stacked.shape[0]
    blocks = size // row_count
    row = lax.broadcasted_iota(jnp.int32, (size, size), 0)
    column = lax.broadcasted_iota(jnp.int32, (size, size), 1)
    same = row // row_count == column // row_count
    short = (row_count, size)
    lane = lax.broadcasted_iota(jnp.int32, (1, size), 1)
    on_diagonal = (
        lax.broadcasted_iota(jnp.int32, short, 0)
        == lax.broadcasted_iota(jnp.int32, short, 1) % row_count
    )
    identity = jnp.where(on_diagonal, 1.0, 0.0).astype(jnp.float32)

    def spread(beside):
        tall = jnp.concatenate([beside] * blocks, axis=0)
        return jnp.where(same, tall, 0.0).astype(jnp.bfloat16)

    def halves(beside):
        high = beside.astype(jnp.bfloat16).astype(jnp.float32)
        return high, beside - high

    def per_block(values):
        total = jnp.zeros((1, size), jnp.float32)
        for b in range(blocks):
            mine = lane // row_count == b
            part = jnp.sum(jnp.where(mine, values, 0.0), axis=1, keepdims=True)
            total = jnp.where(mine, part, total)
        return total

    dot = functools.partial(jnp.dot, preferred_element_type=jnp.float32)
    gram = lax.dot_general(
        stacked, stacked, (((1,), (1,)), ((), ())), preferred_element_type=jnp.float32
    )
    gram = jnp.where(same, gram, 0.0)
    beside = gram[:row_count]
    for b in range(1, blocks):
        beside = beside + gram[b * row_count : (b + 1) * row_count]
    beside = beside * (1.0 / row_count)
    trace_sum = per_block(jnp.sum(beside * identity, axis=0, keepdims=True))
    squares = per_block(jnp.sum(beside * beside, axis=0, keepdims=True))
    damping = (DAMPING / order) * trace_sum
    frobenius = jnp.sqrt(squares + 2.0 * damping * trace_sum + order * damping * damping)
    scale = 1.0 / frobenius
    power = identity - (beside + damping * identity) * scale
    total = identity + power
    for step in range(NS_ITERS):
        high, low = halves(power)
        right_high, right_low = spread(high), spread(low)
        if step == 0:
            left_high, left_low = high.astype(jnp.bfloat16), low.astype(jnp.bfloat16)
        elif step < NS_ITERS - 1:
            total_high, total_low = halves(total)
            left_high = jnp.concatenate([total_high, high], axis=0).astype(jnp.bfloat16)
            left_low = jnp.concatenate([total_low, low], axis=0).astype(jnp.bfloat16)
        else:
            total_high, total_low = halves(total)
            left_high, left_low = total_high.astype(jnp.bfloat16), total_low.astype(jnp.bfloat16)
        product = dot(left_high, right_high) + (
            dot(left_high, right_low) + dot(left_low, right_high)
        )
        if step == 0:
            power = product
        else:
            total = total + product[:row_count]
            power = product[row_count:]
    high, low = halves(total * scale)
    return spread(high), spread(low)


def kernel(
    wide, lengths_hbm, act_ref, grad_ref, in_ref, out_proj_ref, result_ref,
    lengths_ref, act_v, grad_v, in_v, out_v, outgoing, rows_v, work, finished, returned,
    lengths_sem, load_sem, send_sem, recv_sem, back_send_sem, back_recv_sem,
):
    seqs, modules, seq_len, width = act_ref.shape
    rank_in = in_ref.shape[2]
    rank_out = out_proj_ref.shape[2]
    here = rank_out // wide
    all_seqs = seqs * wide
    lanes = BLOCK // rank_in
    blocks = here // lanes
    depth = width // CHUNKS
    me = lax.axis_index("wide")

    def loads(m, c):
        span = pl.ds(c * depth, depth)
        return (
            pltpu.make_async_copy(act_ref.at[:, m, :, span], act_v.at[m, c], load_sem.at[m, c, 0]),
            pltpu.make_async_copy(in_ref.at[m, span, :], in_v.at[m, c], load_sem.at[m, c, 1]),
            pltpu.make_async_copy(grad_ref.at[:, m, :, span], grad_v.at[m, c], load_sem.at[m, c, 2]),
            pltpu.make_async_copy(out_proj_ref.at[m, span, :], out_v.at[m, c], load_sem.at[m, c, 3]),
        )

    lengths_copy = pltpu.make_async_copy(lengths_hbm, lengths_ref, lengths_sem)
    lengths_copy.start()
    for c in range(CHUNKS):
        for copy in loads(0, c):
            copy.start()

    barrier = pltpu.get_barrier_semaphore()

    def greet(d, carry):
        pl.semaphore_signal(
            barrier, inc=1, device_id={"wide": lax.rem(me + d, wide)}, device_id_type=MESH
        )
        return carry

    lax.fori_loop(1, wide, greet, 0)

    def scatter(m, d):
        target = lax.rem(me + d, wide)
        return pltpu.make_async_remote_copy(
            src_ref=outgoing.at[m, target],
            dst_ref=rows_v.at[m, pl.ds(me * seqs, seqs)],
            send_sem=send_sem.at[m, d],
            recv_sem=recv_sem.at[m, d],
            device_id={"wide": target},
            device_id_type=MESH,
        )

    def give_back(m, d):
        target = lax.rem(me + d, wide)
        return pltpu.make_async_remote_copy(
            src_ref=finished.at[m, pl.ds(target * seqs, seqs)],
            dst_ref=returned.at[m, me],
            send_sem=back_send_sem.at[m, d],
            recv_sem=back_recv_sem.at[m, d],
            device_id={"wide": target},
            device_id_type=MESH,
        )

    def each(action):
        def body(i, carry):
            action(wide // 2 + (2 * (i % 2) - 1) * ((i + 1) // 2))
            return carry

        lax.fori_loop(0, wide - 1, body, 0, unroll=5)

    dot = functools.partial(jnp.dot, preferred_element_type=jnp.float32)
    positions = lax.broadcasted_iota(jnp.int32, (seq_len, 1), 0)
    for m in range(modules):
        acc_in = jnp.zeros((seqs * seq_len, rank_in), jnp.float32)
        acc_out = jnp.zeros((seqs * seq_len, rank_out), jnp.float32)
        for c in range(CHUNKS):
            for copy in loads(m, c):
                copy.wait()
            if m + 1 < modules:
                for copy in loads(m + 1, c):
                    copy.start()
            acc_in = acc_in + dot(act_v[m, c].reshape(seqs * seq_len, depth), in_v[m, c])
            acc_out = acc_out + dot(grad_v[m, c].reshape(seqs * seq_len, depth), out_v[m, c])
        if m == 0:
            lengths_copy.wait()
        for s in range(seqs):
            valid = jnp.where(positions < lengths_ref[s], 1.0, 0.0).astype(jnp.float32)
            part = slice(s * seq_len, (s + 1) * seq_len)
            left = (acc_out[part] * valid).astype(jnp.bfloat16)
            right = (acc_in[part] * valid).astype(jnp.bfloat16)
            product = lax.dot_general(
                left, right, (((0,), (0,)), ((), ())), preferred_element_type=jnp.float32
            ) * (1.0 / math.sqrt(seq_len))
            outgoing[m, :, s] = product.astype(jnp.bfloat16).reshape(wide, here, rank_in)
        if m == 0:
            pl.semaphore_wait(barrier, wide - 1)
        each(lambda d: scatter(m, d).start())
        rows_v[m, pl.ds(me * seqs, seqs)] = outgoing[m, me]

    for m in range(modules):
        each(lambda d: scatter(m, d).wait_recv())
        work[...] = rows_v[m].astype(jnp.float32).reshape(all_seqs * here, rank_in)
        stacked = jnp.concatenate(
            [
                jnp.concatenate(
                    [
                        work[pl.ds(b * lanes + j, all_seqs, stride=here), :].astype(jnp.bfloat16)
                        for j in range(lanes)
                    ],
                    axis=1,
                )
                for b in range(blocks)
            ],
            axis=0,
        )
        high, low = polynomial(stacked, BLOCK, all_seqs)
        solved = dot(high, stacked) + dot(low, stacked)
        for b in range(blocks):
            for j in range(lanes):
                work[pl.ds(b * lanes + j, all_seqs, stride=here), :] = solved[
                    b * all_seqs : (b + 1) * all_seqs, j * rank_in : (j + 1) * rank_in
                ]
        finished[m] = work[...].astype(jnp.bfloat16).reshape(all_seqs, here, rank_in)
        each(lambda d: give_back(m, d).start())
        returned[m, me] = finished[m, pl.ds(me * seqs, seqs)]

    for m in range(modules):
        each(lambda d: scatter(m, d).wait_send())
        each(lambda d: give_back(m, d).wait_recv())
        work[...] = returned[m].astype(jnp.float32).reshape(all_seqs * here, rank_in)

        def place(w, carry):
            for o in range(here):
                start = w * (seqs * here) + o
                lane = pl.multiple_of(((m * wide + w) * here + o) * rank_in, rank_in)
                result_ref[:, pl.ds(lane, rank_in)] = work[
                    pl.ds(start, seqs, stride=here), :
                ].astype(jnp.bfloat16)
            return carry

        lax.fori_loop(0, wide, place, 0)
    for m in range(modules):
        each(lambda d: give_back(m, d).wait_send())


def local_fused(wide, activations, out_grads, lengths, proj_in, proj_out):
    seqs, modules, seq_len, width = activations.shape
    rank_in = proj_in.shape[2]
    rank_out = proj_out.shape[2]
    here = rank_out // wide
    depth = width // CHUNKS
    all_seqs = seqs * wide
    hbm = pl.BlockSpec(memory_space=pltpu.HBM)
    bf16 = jnp.bfloat16
    return pl.pallas_call(
        functools.partial(kernel, wide),
        out_shape=pltpu.VMEM((seqs, modules * rank_out * rank_in), bf16),
        in_specs=[hbm] * 5,
        out_specs=pl.BlockSpec(memory_space=pltpu.VMEM),
        scratch_shapes=[
            pltpu.SMEM((seqs,), jnp.int32),
            pltpu.VMEM((modules, CHUNKS, seqs, seq_len, depth), bf16),
            pltpu.VMEM((modules, CHUNKS, seqs, seq_len, depth), bf16),
            pltpu.VMEM((modules, CHUNKS, depth, rank_in), bf16),
            pltpu.VMEM((modules, CHUNKS, depth, rank_out), bf16),
            pltpu.VMEM((modules, wide, seqs, here, rank_in), bf16),
            pltpu.VMEM((modules, all_seqs, here, rank_in), bf16),
            pltpu.VMEM((all_seqs * here, rank_in), jnp.float32),
            pltpu.VMEM((modules, all_seqs, here, rank_in), bf16),
            pltpu.VMEM((modules, wide, seqs, here, rank_in), bf16),
            pltpu.SemaphoreType.DMA,
            pltpu.SemaphoreType.DMA((modules, CHUNKS, 4)),
            pltpu.SemaphoreType.DMA((modules, wide)),
            pltpu.SemaphoreType.DMA((modules, wide)),
            pltpu.SemaphoreType.DMA((modules, wide)),
            pltpu.SemaphoreType.DMA((modules, wide)),
        ],
        compiler_params=pltpu.CompilerParams(
            collective_id=0, has_side_effects=True, vmem_limit_bytes=58 * 1024 * 1024
        ),
    )(lengths, activations, out_grads, proj_in, proj_out)


def solution(mesh):
    in_specs = (
        P(("grp", "wide"), None, None, None),
        P(("grp", "wide"), None, None, None),
        P(("grp", "wide")),
        P(),
        P(),
    )
    out_specs = P(("grp", "wide"), None)
    wide = mesh.shape["wide"]

    def local(activations, out_grads, lengths, proj_in, proj_out):
        here = proj_out.shape[2] // wide
        lanes = BLOCK // proj_in.shape[2]
        stacked = activations.shape[0] * wide * max(here // lanes, 1)
        if here % 16 == 0 and here % lanes == 0 and stacked <= 512:
            return local_fused(wide, activations, out_grads, lengths, proj_in, proj_out)
        return local_plain(activations, out_grads, lengths, proj_in, proj_out)

    return jax.shard_map(
        local, mesh=mesh, in_specs=in_specs, out_specs=out_specs, check_vma=False
    )
```

```python
import functools
import math

import jax
import jax.numpy as jnp
from jax import lax
from jax.experimental import pallas as pl
from jax.experimental.pallas import tpu as pltpu
from jax.sharding import PartitionSpec as P

BLOCK = 512
NS_ITERS = 5
DAMPING = 0.1
CHUNKS = 4
MESH = pl.DeviceIdType.MESH


def precondition(rows):
    row_count = rows.shape[0]
    order = rows.shape[2]
    highest = lax.Precision.HIGHEST
    identity = jnp.eye(row_count, dtype=jnp.float32)[None]
    gram = jnp.einsum("ska,tka->kst", rows, rows, preferred_element_type=jnp.float32) / row_count
    trace_sum = jnp.trace(gram, axis1=1, axis2=2)[:, None, None]
    damping = DAMPING * trace_sum / order
    squares = jnp.sum(gram * gram, axis=(1, 2), keepdims=True)
    frobenius = jnp.sqrt(squares + 2.0 * damping * trace_sum + order * damping * damping)
    power = identity - (gram + damping * identity) / frobenius
    total = identity + power
    for _ in range(NS_ITERS - 1):
        power = jnp.einsum("kab,kbc->kac", power, power, precision=highest)
        total = total + jnp.einsum("kab,kbc->kac", total, power, precision=highest)
    return jnp.einsum(
        "kst,tka->ska", total / frobenius, rows.astype(jnp.float32), precision=highest
    ).astype(jnp.bfloat16)


def local_plain(activations, out_grads, lengths, proj_in, proj_out):
    seq_count, module_count, seq_len, model_width = activations.shape
    rank_in = proj_in.shape[2]
    rank_out = proj_out.shape[2]
    acc_in = jnp.einsum("smtd,mdr->smtr", activations, proj_in, preferred_element_type=jnp.float32)
    acc_out = jnp.einsum("smtd,mdr->smtr", out_grads, proj_out, preferred_element_type=jnp.float32)
    positions = lax.broadcasted_iota(jnp.int32, (seq_count, seq_len), 1)
    valid_mask = (positions < lengths[:, None]).astype(jnp.float32)[:, None, :, None]
    projected_in = (acc_in * valid_mask).astype(jnp.bfloat16)
    projected_out = (acc_out * valid_mask).astype(jnp.bfloat16)
    seq_grads = jnp.einsum(
        "smto,smti->smoi", projected_out, projected_in, preferred_element_type=jnp.float32
    ) * (1.0 / math.sqrt(seq_len))
    grad_size = module_count * rank_out * rank_in
    wide_count = lax.axis_size("wide")
    blocks_here = grad_size // (BLOCK * wide_count)
    blocks = seq_grads.astype(jnp.bfloat16).reshape(seq_count, wide_count, blocks_here, BLOCK)
    owned_rows = lax.all_to_all(blocks, "wide", split_axis=1, concat_axis=0, tiled=True)
    result = precondition(owned_rows[:, 0])[:, None]
    returned = lax.all_to_all(result, "wide", split_axis=0, concat_axis=1, tiled=True)
    return returned.reshape(seq_count, grad_size)


def polynomial(stacked, order, row_count):
    size = stacked.shape[0]
    blocks = size // row_count
    row = lax.broadcasted_iota(jnp.int32, (size, size), 0)
    column = lax.broadcasted_iota(jnp.int32, (size, size), 1)
    same = row // row_count == column // row_count
    short = (row_count, size)
    lane = lax.broadcasted_iota(jnp.int32, (1, size), 1)
    on_diagonal = (
        lax.broadcasted_iota(jnp.int32, short, 0)
        == lax.broadcasted_iota(jnp.int32, short, 1) % row_count
    )
    identity = jnp.where(on_diagonal, 1.0, 0.0).astype(jnp.float32)

    def spread(beside):
        tall = jnp.concatenate([beside] * blocks, axis=0)
        return jnp.where(same, tall, 0.0).astype(jnp.bfloat16)

    def halves(beside):
        high = beside.astype(jnp.bfloat16).astype(jnp.float32)
        return high, beside - high

    def per_block(values):
        total = jnp.zeros((1, size), jnp.float32)
        for b in range(blocks):
            mine = lane // row_count == b
            part = jnp.sum(jnp.where(mine, values, 0.0), axis=1, keepdims=True)
            total = jnp.where(mine, part, total)
        return total

    dot = functools.partial(jnp.dot, preferred_element_type=jnp.float32)
    gram = lax.dot_general(
        stacked, stacked, (((1,), (1,)), ((), ())), preferred_element_type=jnp.float32
    )
    gram = jnp.where(same, gram, 0.0)
    beside = gram[:row_count]
    for b in range(1, blocks):
        beside = beside + gram[b * row_count : (b + 1) * row_count]
    beside = beside * (1.0 / row_count)
    trace_sum = per_block(jnp.sum(beside * identity, axis=0, keepdims=True))
    squares = per_block(jnp.sum(beside * beside, axis=0, keepdims=True))
    damping = (DAMPING / order) * trace_sum
    frobenius = jnp.sqrt(squares + 2.0 * damping * trace_sum + order * damping * damping)
    scale = 1.0 / frobenius
    power = identity - (beside + damping * identity) * scale
    total = identity + power
    for step in range(NS_ITERS):
        high, low = halves(power)
        right_high, right_low = spread(high), spread(low)
        if step == 0:
            left_high, left_low = high.astype(jnp.bfloat16), low.astype(jnp.bfloat16)
        elif step < NS_ITERS - 1:
            total_high, total_low = halves(total)
            left_high = jnp.concatenate([total_high, high], axis=0).astype(jnp.bfloat16)
            left_low = jnp.concatenate([total_low, low], axis=0).astype(jnp.bfloat16)
        else:
            total_high, total_low = halves(total)
            left_high, left_low = total_high.astype(jnp.bfloat16), total_low.astype(jnp.bfloat16)
        product = dot(left_high, right_high) + (
            dot(left_high, right_low) + dot(left_low, right_high)
        )
        if step == 0:
            power = product
        else:
            total = total + product[:row_count]
            power = product[row_count:]
    high, low = halves(total * scale)
    return spread(high), spread(low)


def kernel(
    wide, lengths_hbm, act_ref, grad_ref, in_ref, out_proj_ref, result_ref,
    lengths_ref, act_v, grad_v, in_v, out_v, inputs, outgoing, incoming, work, finished, returned,
    lengths_sem, load_sem, send_sem, recv_sem, back_send_sem, back_recv_sem,
    far_send_sem, far_recv_sem, pair_send_sem, pair_recv_sem, core_send_sem, core_recv_sem,
):
    seqs, modules, seq_len, width = act_ref.shape
    rank_in = in_ref.shape[2]
    rank_out = out_proj_ref.shape[2]
    here = rank_out // wide
    tokens = seqs * seq_len
    all_seqs = seqs * wide
    lanes = BLOCK // rank_in
    blocks = here // lanes
    depth = width // CHUNKS
    quads = wide // 4
    me = lax.axis_index("wide")
    quad, rank = me // 4, lax.rem(me, 4)
    pair_rank = lax.rem(rank + 2, 4)
    sibling = me + 1 - 2 * lax.rem(me, 2)

    def loads(m, side, c):
        span = pl.ds(c * depth, depth)
        source, projector = ((act_ref, in_ref), (grad_ref, out_proj_ref))[side]
        source_v, projector_v = ((act_v, in_v), (grad_v, out_v))[side]
        return (
            pltpu.make_async_copy(
                source.at[:, m, :, span], source_v.at[m, c], load_sem.at[m, c, 2 * side]
            ),
            pltpu.make_async_copy(
                projector.at[m, span, :], projector_v.at[m, c], load_sem.at[m, c, 2 * side + 1]
            ),
        )

    stages = [(m, side) for m in range(modules) for side in range(2)]
    lengths_copy = pltpu.make_async_copy(lengths_hbm, lengths_ref, lengths_sem)
    lengths_copy.start()
    for stage in stages[:2]:
        for c in range(CHUNKS):
            for copy in loads(*stage, c):
                copy.start()

    barrier = pltpu.get_barrier_semaphore()

    def greet(d, carry):
        pl.semaphore_signal(
            barrier, inc=1, device_id={"wide": lax.rem(me + d, wide)}, device_id_type=MESH
        )
        return carry

    lax.fori_loop(1, wide, greet, 0)

    def hand(m, slot, target, send, recv):
        return pltpu.make_async_remote_copy(
            src_ref=inputs.at[m, slot],
            dst_ref=inputs.at[m, slot],
            send_sem=send,
            recv_sem=recv,
            device_id={"wide": target},
            device_id_type=MESH,
        )

    def origin(k, of_rank):
        return lax.rem(quad + quads - k, quads) * 4 + of_rank

    def to_quad(m, j):
        target = lax.rem(quad + j, quads) * 4 + rank
        return hand(m, me, target, far_send_sem.at[m, j], far_recv_sem.at[m, j])

    def to_pair(m, k):
        target = quad * 4 + pair_rank
        return hand(m, origin(k, rank), target, pair_send_sem.at[m, k], pair_recv_sem.at[m, k])

    def to_core(m, k):
        slot = origin(k, rank) if k < quads else origin(k - quads, pair_rank)
        return hand(m, slot, sibling, core_send_sem.at[m, k], core_recv_sem.at[m, k])

    def scatter(m, d):
        target = lax.rem(me + d, wide)
        return pltpu.make_async_remote_copy(
            src_ref=outgoing.at[m, target],
            dst_ref=incoming.at[m, me],
            send_sem=send_sem.at[m, d],
            recv_sem=recv_sem.at[m, d],
            device_id={"wide": target},
            device_id_type=MESH,
        )

    def give_back(m, d):
        target = lax.rem(me + d, wide)
        return pltpu.make_async_remote_copy(
            src_ref=finished.at[m, pl.ds(target * seqs, seqs)],
            dst_ref=returned.at[m, me],
            send_sem=back_send_sem.at[m, d],
            recv_sem=back_recv_sem.at[m, d],
            device_id={"wide": target},
            device_id_type=MESH,
        )

    def each(action):
        def body(i, carry):
            action(wide // 2 + (2 * (i % 2) - 1) * ((i + 1) // 2))
            return carry

        lax.fori_loop(0, wide - 1, body, 0, unroll=5)

    def hand_on(m):
        for j in range(1, quads):
            to_quad(m, j).wait_recv()
            to_pair(m, j).start()
            to_core(m, j).start()

    dot = functools.partial(jnp.dot, preferred_element_type=jnp.float32)
    positions = lax.broadcasted_iota(jnp.int32, (seq_len, 1), 0)

    def valid():
        return jnp.concatenate(
            [
                jnp.where(positions < lengths_ref[s], 1.0, 0.0).astype(jnp.float32)
                for s in range(seqs)
            ],
            axis=0,
        )

    for index, (m, side) in enumerate(stages):
        source_v, projector_v = ((act_v, in_v), (grad_v, out_v))[side]
        total = jnp.zeros((tokens, (rank_in, rank_out)[side]), jnp.float32)
        for c in range(CHUNKS):
            for copy in loads(m, side, c):
                copy.wait()
            if index + 2 < len(stages):
                for copy in loads(*stages[index + 2], c):
                    copy.start()
            total = total + dot(source_v[m, c].reshape(tokens, depth), projector_v[m, c])
        if index == 0:
            lengths_copy.wait()
        total = total * valid()
        if side == 0:
            inputs[m, me] = total.astype(jnp.bfloat16)
            if index == 0:
                pl.semaphore_wait(barrier, wide - 1)
            for j in range(1, quads):
                to_quad(m, j).start()
            to_pair(m, 0).start()
            to_core(m, 0).start()
        else:
            outgoing[m] = total.T.astype(jnp.bfloat16).reshape(wide, here, tokens)
            each(lambda d: scatter(m, d).start())
            incoming[m, me] = outgoing[m, me]

    own_tokens = (
        lax.broadcasted_iota(jnp.int32, (seqs * here, tokens), 0) // here
        == lax.broadcasted_iota(jnp.int32, (seqs * here, tokens), 1) // seq_len
    )
    hand_on(0)
    for m in range(modules):
        for k in range(quads):
            to_pair(m, k).wait_recv()
            to_core(m, quads + k).start()
        each(lambda d: scatter(m, d).wait_recv())
        for k in range(2 * quads):
            to_core(m, k).wait_recv()
        for w in range(wide):
            left = jnp.concatenate([incoming[m, w].astype(jnp.float32)] * seqs, axis=0)
            left = jnp.where(own_tokens, left, 0.0).astype(jnp.bfloat16)
            work[w * seqs * here : (w + 1) * seqs * here, :] = dot(left, inputs[m, w]) * (
                1.0 / math.sqrt(seq_len)
            )
        stacked = jnp.concatenate(
            [
                jnp.concatenate(
                    [
                        work[pl.ds(b * lanes + j, all_seqs, stride=here), :].astype(jnp.bfloat16)
                        for j in range(lanes)
                    ],
                    axis=1,
                )
                for b in range(blocks)
            ],
            axis=0,
        )
        high, low = polynomial(stacked, BLOCK, all_seqs)
        solved = dot(high, stacked) + dot(low, stacked)
        if m + 1 < modules:
            hand_on(m + 1)
        for b in range(blocks):
            for j in range(lanes):
                work[pl.ds(b * lanes + j, all_seqs, stride=here), :] = solved[
                    b * all_seqs : (b + 1) * all_seqs, j * rank_in : (j + 1) * rank_in
                ]
        finished[m] = work[...].astype(jnp.bfloat16).reshape(all_seqs, here, rank_in)
        each(lambda d: give_back(m, d).start())
        returned[m, me] = finished[m, pl.ds(me * seqs, seqs)]

    for m in range(modules):
        each(lambda d: scatter(m, d).wait_send())
        for j in range(1, quads):
            to_quad(m, j).wait_send()
        for k in range(quads):
            to_pair(m, k).wait_send()
        for k in range(2 * quads):
            to_core(m, k).wait_send()
        each(lambda d: give_back(m, d).wait_recv())
        work[...] = returned[m].astype(jnp.float32).reshape(all_seqs * here, rank_in)

        def place(w, carry):
            for o in range(here):
                start = w * (seqs * here) + o
                lane = pl.multiple_of(((m * wide + w) * here + o) * rank_in, rank_in)
                result_ref[:, pl.ds(lane, rank_in)] = work[
                    pl.ds(start, seqs, stride=here), :
                ].astype(jnp.bfloat16)
            return carry

        lax.fori_loop(0, wide, place, 0)
    for m in range(modules):
        each(lambda d: give_back(m, d).wait_send())


def local_fused(wide, activations, out_grads, lengths, proj_in, proj_out):
    seqs, modules, seq_len, width = activations.shape
    rank_in = proj_in.shape[2]
    rank_out = proj_out.shape[2]
    here = rank_out // wide
    depth = width // CHUNKS
    all_seqs = seqs * wide
    hbm = pl.BlockSpec(memory_space=pltpu.HBM)
    bf16 = jnp.bfloat16
    return pl.pallas_call(
        functools.partial(kernel, wide),
        out_shape=pltpu.VMEM((seqs, modules * rank_out * rank_in), bf16),
        in_specs=[hbm] * 5,
        out_specs=pl.BlockSpec(memory_space=pltpu.VMEM),
        scratch_shapes=[
            pltpu.SMEM((seqs,), jnp.int32),
            pltpu.VMEM((modules, CHUNKS, seqs, seq_len, depth), bf16),
            pltpu.VMEM((modules, CHUNKS, seqs, seq_len, depth), bf16),
            pltpu.VMEM((modules, CHUNKS, depth, rank_in), bf16),
            pltpu.VMEM((modules, CHUNKS, depth, rank_out), bf16),
            pltpu.VMEM((modules, wide, seqs * seq_len, rank_in), bf16),
            pltpu.VMEM((modules, wide, here, seqs * seq_len), bf16),
            pltpu.VMEM((modules, wide, here, seqs * seq_len), bf16),
            pltpu.VMEM((all_seqs * here, rank_in), jnp.float32),
            pltpu.VMEM((modules, all_seqs, here, rank_in), bf16),
            pltpu.VMEM((modules, wide, seqs, here, rank_in), bf16),
            pltpu.SemaphoreType.DMA,
            pltpu.SemaphoreType.DMA((modules, CHUNKS, 4)),
            pltpu.SemaphoreType.DMA((modules, wide)),
            pltpu.SemaphoreType.DMA((modules, wide)),
            pltpu.SemaphoreType.DMA((modules, wide)),
            pltpu.SemaphoreType.DMA((modules, wide)),
            pltpu.SemaphoreType.DMA((modules, wide // 4)),
            pltpu.SemaphoreType.DMA((modules, wide // 4)),
            pltpu.SemaphoreType.DMA((modules, wide // 4)),
            pltpu.SemaphoreType.DMA((modules, wide // 4)),
            pltpu.SemaphoreType.DMA((modules, wide // 2)),
            pltpu.SemaphoreType.DMA((modules, wide // 2)),
        ],
        compiler_params=pltpu.CompilerParams(
            collective_id=0, has_side_effects=True, vmem_limit_bytes=58 * 1024 * 1024
        ),
    )(lengths, activations, out_grads, proj_in, proj_out)


def solution(mesh):
    in_specs = (
        P(("grp", "wide"), None, None, None),
        P(("grp", "wide"), None, None, None),
        P(("grp", "wide")),
        P(),
        P(),
    )
    out_specs = P(("grp", "wide"), None)
    wide = mesh.shape["wide"]

    def local(activations, out_grads, lengths, proj_in, proj_out):
        here = proj_out.shape[2] // wide
        lanes = BLOCK // proj_in.shape[2]
        stacked = activations.shape[0] * wide * max(here // lanes, 1)
        tokens = activations.shape[0] * activations.shape[2]
        whole_tiles = here % 16 == 0 and here % lanes == 0 and tokens % 128 == 0
        if whole_tiles and wide % 4 == 0 and stacked <= 512:
            return local_fused(wide, activations, out_grads, lengths, proj_in, proj_out)
        return local_plain(activations, out_grads, lengths, proj_in, proj_out)

    return jax.shard_map(
        local, mesh=mesh, in_specs=in_specs, out_specs=out_specs, check_vma=False
    )
```

```python
import functools
import math

import jax
import jax.numpy as jnp
from jax import lax
from jax.experimental import pallas as pl
from jax.experimental.pallas import tpu as pltpu
from jax.sharding import PartitionSpec as P

BLOCK = 512
NS_ITERS = 5
DAMPING = 0.1
CHUNKS = 4
MESH = pl.DeviceIdType.MESH


def precondition(rows):
    row_count = rows.shape[0]
    order = rows.shape[2]
    highest = lax.Precision.HIGHEST
    identity = jnp.eye(row_count, dtype=jnp.float32)[None]
    gram = jnp.einsum("ska,tka->kst", rows, rows, preferred_element_type=jnp.float32) / row_count
    trace_sum = jnp.trace(gram, axis1=1, axis2=2)[:, None, None]
    damping = DAMPING * trace_sum / order
    squares = jnp.sum(gram * gram, axis=(1, 2), keepdims=True)
    frobenius = jnp.sqrt(squares + 2.0 * damping * trace_sum + order * damping * damping)
    power = identity - (gram + damping * identity) / frobenius
    total = identity + power
    for _ in range(NS_ITERS - 1):
        power = jnp.einsum("kab,kbc->kac", power, power, precision=highest)
        total = total + jnp.einsum("kab,kbc->kac", total, power, precision=highest)
    return jnp.einsum(
        "kst,tka->ska", total / frobenius, rows.astype(jnp.float32), precision=highest
    ).astype(jnp.bfloat16)


def local_plain(activations, out_grads, lengths, proj_in, proj_out):
    seq_count, module_count, seq_len, model_width = activations.shape
    rank_in = proj_in.shape[2]
    rank_out = proj_out.shape[2]
    acc_in = jnp.einsum("smtd,mdr->smtr", activations, proj_in, preferred_element_type=jnp.float32)
    acc_out = jnp.einsum("smtd,mdr->smtr", out_grads, proj_out, preferred_element_type=jnp.float32)
    positions = lax.broadcasted_iota(jnp.int32, (seq_count, seq_len), 1)
    valid_mask = (positions < lengths[:, None]).astype(jnp.float32)[:, None, :, None]
    projected_in = (acc_in * valid_mask).astype(jnp.bfloat16)
    projected_out = (acc_out * valid_mask).astype(jnp.bfloat16)
    seq_grads = jnp.einsum(
        "smto,smti->smoi", projected_out, projected_in, preferred_element_type=jnp.float32
    ) * (1.0 / math.sqrt(seq_len))
    grad_size = module_count * rank_out * rank_in
    wide_count = lax.axis_size("wide")
    blocks_here = grad_size // (BLOCK * wide_count)
    blocks = seq_grads.astype(jnp.bfloat16).reshape(seq_count, wide_count, blocks_here, BLOCK)
    owned_rows = lax.all_to_all(blocks, "wide", split_axis=1, concat_axis=0, tiled=True)
    result = precondition(owned_rows[:, 0])[:, None]
    returned = lax.all_to_all(result, "wide", split_axis=0, concat_axis=1, tiled=True)
    return returned.reshape(seq_count, grad_size)


def polynomial(stacked, order, row_count):
    size = stacked.shape[0]
    blocks = size // row_count
    row = lax.broadcasted_iota(jnp.int32, (size, size), 0)
    column = lax.broadcasted_iota(jnp.int32, (size, size), 1)
    same = row // row_count == column // row_count
    short = (row_count, size)
    lane = lax.broadcasted_iota(jnp.int32, (1, size), 1)
    on_diagonal = (
        lax.broadcasted_iota(jnp.int32, short, 0)
        == lax.broadcasted_iota(jnp.int32, short, 1) % row_count
    )
    identity = jnp.where(on_diagonal, 1.0, 0.0).astype(jnp.float32)

    def spread(beside):
        tall = jnp.concatenate([beside] * blocks, axis=0)
        return jnp.where(same, tall, 0.0).astype(jnp.bfloat16)

    def halves(beside):
        high = beside.astype(jnp.bfloat16).astype(jnp.float32)
        return high, beside - high

    def per_block(values):
        total = jnp.zeros((1, size), jnp.float32)
        for b in range(blocks):
            mine = lane // row_count == b
            part = jnp.sum(jnp.where(mine, values, 0.0), axis=1, keepdims=True)
            total = jnp.where(mine, part, total)
        return total

    dot = functools.partial(jnp.dot, preferred_element_type=jnp.float32)
    gram = lax.dot_general(
        stacked, stacked, (((1,), (1,)), ((), ())), preferred_element_type=jnp.float32
    )
    gram = jnp.where(same, gram, 0.0)
    beside = gram[:row_count]
    for b in range(1, blocks):
        beside = beside + gram[b * row_count : (b + 1) * row_count]
    beside = beside * (1.0 / row_count)
    trace_sum = per_block(jnp.sum(beside * identity, axis=0, keepdims=True))
    squares = per_block(jnp.sum(beside * beside, axis=0, keepdims=True))
    damping = (DAMPING / order) * trace_sum
    frobenius = jnp.sqrt(squares + 2.0 * damping * trace_sum + order * damping * damping)
    scale = 1.0 / frobenius
    power = identity - (beside + damping * identity) * scale
    total = identity + power
    for step in range(NS_ITERS):
        high, low = halves(power)
        right_high, right_low = spread(high), spread(low)
        if step == 0:
            left_high, left_low = high.astype(jnp.bfloat16), low.astype(jnp.bfloat16)
        elif step < NS_ITERS - 1:
            total_high, total_low = halves(total)
            left_high = jnp.concatenate([total_high, high], axis=0).astype(jnp.bfloat16)
            left_low = jnp.concatenate([total_low, low], axis=0).astype(jnp.bfloat16)
        else:
            total_high, total_low = halves(total)
            left_high, left_low = total_high.astype(jnp.bfloat16), total_low.astype(jnp.bfloat16)
        product = dot(left_high, right_high) + (
            dot(left_high, right_low) + dot(left_low, right_high)
        )
        if step == 0:
            power = product
        else:
            total = total + product[:row_count]
            power = product[row_count:]
    high, low = halves(total * scale)
    return spread(high), spread(low)


def kernel(
    wide, lengths_hbm, act_ref, grad_ref, in_ref, out_proj_ref, result_ref,
    lengths_ref, act_v, grad_v, in_v, out_v, outgoing, rows_v, work, finished, returned,
    lengths_sem, load_sem, send_sem, recv_sem, back_send_sem, back_recv_sem,
):
    seqs, modules, seq_len, width = act_ref.shape
    rank_in = in_ref.shape[2]
    rank_out = out_proj_ref.shape[2]
    here = rank_out // wide
    all_seqs = seqs * wide
    lanes = BLOCK // rank_in
    blocks = here // lanes
    depth = width // CHUNKS
    me = lax.axis_index("wide")

    def loads(m, c):
        span = pl.ds(c * depth, depth)
        return (
            pltpu.make_async_copy(act_ref.at[:, m, :, span], act_v.at[m, c], load_sem.at[m, c, 0]),
            pltpu.make_async_copy(in_ref.at[m, span, :], in_v.at[m, c], load_sem.at[m, c, 1]),
            pltpu.make_async_copy(grad_ref.at[:, m, :, span], grad_v.at[m, c], load_sem.at[m, c, 2]),
            pltpu.make_async_copy(out_proj_ref.at[m, span, :], out_v.at[m, c], load_sem.at[m, c, 3]),
        )

    lengths_copy = pltpu.make_async_copy(lengths_hbm, lengths_ref, lengths_sem)
    lengths_copy.start()
    for c in range(CHUNKS):
        for copy in loads(0, c):
            copy.start()

    barrier = pltpu.get_barrier_semaphore()

    def greet(d, carry):
        pl.semaphore_signal(
            barrier, inc=1, device_id={"wide": lax.rem(me + d, wide)}, device_id_type=MESH
        )
        return carry

    lax.fori_loop(1, wide, greet, 0, unroll=5)

    def scatter(m, d):
        target = lax.rem(me + d, wide)
        return pltpu.make_async_remote_copy(
            src_ref=outgoing.at[m, target],
            dst_ref=rows_v.at[m, pl.ds(me * seqs, seqs)],
            send_sem=send_sem.at[m],
            recv_sem=recv_sem.at[m],
            device_id={"wide": target},
            device_id_type=MESH,
        )

    def give_back(m, d):
        target = lax.rem(me + d, wide)
        return pltpu.make_async_remote_copy(
            src_ref=finished.at[m, pl.ds(target * seqs, seqs)],
            dst_ref=returned.at[m, me],
            send_sem=back_send_sem.at[m],
            recv_sem=back_recv_sem.at[m, d],
            device_id={"wide": target},
            device_id_type=MESH,
        )

    def all_others(buffer, m, send, recv):
        part = buffer.at[m, pl.ds(0, (wide - 1) * seqs)]
        return pltpu.make_async_remote_copy(
            src_ref=part,
            dst_ref=part,
            send_sem=send,
            recv_sem=recv,
            device_id={"wide": lax.rem(me + 1, wide)},
            device_id_type=MESH,
        )

    def each(action):
        def body(i, carry):
            action(wide // 2 + (2 * (i % 2) - 1) * ((i + 1) // 2))
            return carry

        lax.fori_loop(0, wide - 1, body, 0, unroll=5)

    dot = functools.partial(jnp.dot, preferred_element_type=jnp.float32)
    positions = lax.broadcasted_iota(jnp.int32, (seq_len, 1), 0)
    for m in range(modules):
        acc_in = jnp.zeros((seqs * seq_len, rank_in), jnp.float32)
        acc_out = jnp.zeros((seqs * seq_len, rank_out), jnp.float32)
        for c in range(CHUNKS):
            for copy in loads(m, c):
                copy.wait()
            if m + 1 < modules:
                for copy in loads(m + 1, c):
                    copy.start()
            acc_in = acc_in + dot(act_v[m, c].reshape(seqs * seq_len, depth), in_v[m, c])
            acc_out = acc_out + dot(grad_v[m, c].reshape(seqs * seq_len, depth), out_v[m, c])
        if m == 0:
            lengths_copy.wait()
        for s in range(seqs):
            valid = jnp.where(positions < lengths_ref[s], 1.0, 0.0).astype(jnp.float32)
            part = slice(s * seq_len, (s + 1) * seq_len)
            left = (acc_out[part] * valid).astype(jnp.bfloat16)
            right = (acc_in[part] * valid).astype(jnp.bfloat16)
            product = lax.dot_general(
                left, right, (((0,), (0,)), ((), ())), preferred_element_type=jnp.float32
            ) * (1.0 / math.sqrt(seq_len))
            outgoing[m, :, s] = product.astype(jnp.bfloat16).reshape(wide, here, rank_in)
        if m == 0:
            pl.semaphore_wait(barrier, wide - 1)
        each(lambda d: scatter(m, d).start())
        rows_v[m, pl.ds(me * seqs, seqs)] = outgoing[m, me]

    for m in range(modules):
        all_others(rows_v, m, send_sem.at[m], recv_sem.at[m]).wait_recv()
        work[...] = rows_v[m].astype(jnp.float32).reshape(all_seqs * here, rank_in)
        stacked = jnp.concatenate(
            [
                jnp.concatenate(
                    [
                        work[pl.ds(b * lanes + j, all_seqs, stride=here), :].astype(jnp.bfloat16)
                        for j in range(lanes)
                    ],
                    axis=1,
                )
                for b in range(blocks)
            ],
            axis=0,
        )
        high, low = polynomial(stacked, BLOCK, all_seqs)
        solved = dot(high, stacked) + dot(low, stacked)
        for b in range(blocks):
            for j in range(lanes):
                work[pl.ds(b * lanes + j, all_seqs, stride=here), :] = solved[
                    b * all_seqs : (b + 1) * all_seqs, j * rank_in : (j + 1) * rank_in
                ]
        finished[m] = work[...].astype(jnp.bfloat16).reshape(all_seqs, here, rank_in)
        each(lambda d: give_back(m, d).start())
        returned[m, me] = finished[m, pl.ds(me * seqs, seqs)]

    def place(m, w):
        rows = seqs * here
        top = pl.multiple_of(w * rows, rows)
        work[pl.ds(top, rows), :] = returned[m, w].astype(jnp.float32).reshape(rows, rank_in)
        for o in range(here):
            lane = pl.multiple_of(((m * wide + w) * here + o) * rank_in, rank_in)
            result_ref[:, pl.ds(lane, rank_in)] = work[
                pl.ds(top + o, seqs, stride=here), :
            ].astype(jnp.bfloat16)

    for m in range(modules):
        all_others(rows_v, m, send_sem.at[m], recv_sem.at[m]).wait_send()
        place(m, me)
    for m in range(modules):

        def take(i, carry):
            d = wide // 2 + (2 * (i % 2) - 1) * ((i + 1) // 2)
            give_back(m, d).wait_recv()
            place(m, lax.rem(me + wide - d, wide))
            return carry

        lax.fori_loop(0, wide - 1, take, 0)
    for m in range(modules):
        all_others(finished, m, back_send_sem.at[m], recv_sem.at[m]).wait_send()


def local_fused(wide, activations, out_grads, lengths, proj_in, proj_out):
    seqs, modules, seq_len, width = activations.shape
    rank_in = proj_in.shape[2]
    rank_out = proj_out.shape[2]
    here = rank_out // wide
    depth = width // CHUNKS
    all_seqs = seqs * wide
    hbm = pl.BlockSpec(memory_space=pltpu.HBM)
    bf16 = jnp.bfloat16
    return pl.pallas_call(
        functools.partial(kernel, wide),
        out_shape=pltpu.VMEM((seqs, modules * rank_out * rank_in), bf16),
        in_specs=[hbm] * 5,
        out_specs=pl.BlockSpec(memory_space=pltpu.VMEM),
        scratch_shapes=[
            pltpu.SMEM((seqs,), jnp.int32),
            pltpu.VMEM((modules, CHUNKS, seqs, seq_len, depth), bf16),
            pltpu.VMEM((modules, CHUNKS, seqs, seq_len, depth), bf16),
            pltpu.VMEM((modules, CHUNKS, depth, rank_in), bf16),
            pltpu.VMEM((modules, CHUNKS, depth, rank_out), bf16),
            pltpu.VMEM((modules, wide, seqs, here, rank_in), bf16),
            pltpu.VMEM((modules, all_seqs, here, rank_in), bf16),
            pltpu.VMEM((all_seqs * here, rank_in), jnp.float32),
            pltpu.VMEM((modules, all_seqs, here, rank_in), bf16),
            pltpu.VMEM((modules, wide, seqs, here, rank_in), bf16),
            pltpu.SemaphoreType.DMA,
            pltpu.SemaphoreType.DMA((modules, CHUNKS, 4)),
            pltpu.SemaphoreType.DMA((modules,)),
            pltpu.SemaphoreType.DMA((modules,)),
            pltpu.SemaphoreType.DMA((modules,)),
            pltpu.SemaphoreType.DMA((modules, wide)),
        ],
        compiler_params=pltpu.CompilerParams(
            collective_id=0, has_side_effects=True, vmem_limit_bytes=58 * 1024 * 1024
        ),
    )(lengths, activations, out_grads, proj_in, proj_out)


def solution(mesh):
    in_specs = (
        P(("grp", "wide"), None, None, None),
        P(("grp", "wide"), None, None, None),
        P(("grp", "wide")),
        P(),
        P(),
    )
    out_specs = P(("grp", "wide"), None)
    wide = mesh.shape["wide"]

    def local(activations, out_grads, lengths, proj_in, proj_out):
        here = proj_out.shape[2] // wide
        lanes = BLOCK // proj_in.shape[2]
        stacked = activations.shape[0] * wide * max(here // lanes, 1)
        if here % 16 == 0 and here % lanes == 0 and stacked <= 512:
            return local_fused(wide, activations, out_grads, lengths, proj_in, proj_out)
        return local_plain(activations, out_grads, lengths, proj_in, proj_out)

    return jax.shard_map(
        local, mesh=mesh, in_specs=in_specs, out_specs=out_specs, check_vma=False
    )
```

```python
import functools
import math

import jax
import jax.numpy as jnp
from jax import lax
from jax.experimental import pallas as pl
from jax.experimental.pallas import tpu as pltpu
from jax.sharding import PartitionSpec as P

BLOCK = 512
NS_ITERS = 5
DAMPING = 0.1
CHUNKS = 4
MESH = pl.DeviceIdType.MESH


def precondition(rows):
    row_count = rows.shape[0]
    order = rows.shape[2]
    highest = lax.Precision.HIGHEST
    identity = jnp.eye(row_count, dtype=jnp.float32)[None]
    gram = jnp.einsum("ska,tka->kst", rows, rows, preferred_element_type=jnp.float32) / row_count
    trace_sum = jnp.trace(gram, axis1=1, axis2=2)[:, None, None]
    damping = DAMPING * trace_sum / order
    squares = jnp.sum(gram * gram, axis=(1, 2), keepdims=True)
    frobenius = jnp.sqrt(squares + 2.0 * damping * trace_sum + order * damping * damping)
    power = identity - (gram + damping * identity) / frobenius
    total = identity + power
    for _ in range(NS_ITERS - 1):
        power = jnp.einsum("kab,kbc->kac", power, power, precision=highest)
        total = total + jnp.einsum("kab,kbc->kac", total, power, precision=highest)
    return jnp.einsum(
        "kst,tka->ska", total / frobenius, rows.astype(jnp.float32), precision=highest
    ).astype(jnp.bfloat16)


def local_plain(activations, out_grads, lengths, proj_in, proj_out):
    seq_count, module_count, seq_len, model_width = activations.shape
    rank_in = proj_in.shape[2]
    rank_out = proj_out.shape[2]
    acc_in = jnp.einsum("smtd,mdr->smtr", activations, proj_in, preferred_element_type=jnp.float32)
    acc_out = jnp.einsum("smtd,mdr->smtr", out_grads, proj_out, preferred_element_type=jnp.float32)
    positions = lax.broadcasted_iota(jnp.int32, (seq_count, seq_len), 1)
    valid_mask = (positions < lengths[:, None]).astype(jnp.float32)[:, None, :, None]
    projected_in = (acc_in * valid_mask).astype(jnp.bfloat16)
    projected_out = (acc_out * valid_mask).astype(jnp.bfloat16)
    seq_grads = jnp.einsum(
        "smto,smti->smoi", projected_out, projected_in, preferred_element_type=jnp.float32
    ) * (1.0 / math.sqrt(seq_len))
    grad_size = module_count * rank_out * rank_in
    wide_count = lax.axis_size("wide")
    blocks_here = grad_size // (BLOCK * wide_count)
    blocks = seq_grads.astype(jnp.bfloat16).reshape(seq_count, wide_count, blocks_here, BLOCK)
    owned_rows = lax.all_to_all(blocks, "wide", split_axis=1, concat_axis=0, tiled=True)
    result = precondition(owned_rows[:, 0])[:, None]
    returned = lax.all_to_all(result, "wide", split_axis=0, concat_axis=1, tiled=True)
    return returned.reshape(seq_count, grad_size)


def block_masks(size, row_count):
    row = lax.broadcasted_iota(jnp.int32, (size, size), 0)
    column = lax.broadcasted_iota(jnp.int32, (size, size), 1)
    mask = jnp.where(row // row_count == column // row_count, 1.0, 0.0).astype(jnp.bfloat16)
    short = (row_count, size)
    on_diagonal = (
        lax.broadcasted_iota(jnp.int32, short, 0)
        == lax.broadcasted_iota(jnp.int32, short, 1) % row_count
    )
    return mask, jnp.where(on_diagonal, 1.0, 0.0).astype(jnp.float32)


def polynomial(stacked, order, row_count, masks):
    size = stacked.shape[0]
    blocks = size // row_count
    mask, identity = masks
    lane = lax.broadcasted_iota(jnp.int32, (1, size), 1)

    def spread(beside):
        return jnp.concatenate([beside.astype(jnp.bfloat16)] * blocks, axis=0) * mask

    def halves(beside):
        high = beside.astype(jnp.bfloat16).astype(jnp.float32)
        return high, beside - high

    def per_block(values):
        total = jnp.zeros((1, size), jnp.float32)
        for b in range(blocks):
            mine = lane // row_count == b
            part = jnp.sum(jnp.where(mine, values, 0.0), axis=1, keepdims=True)
            total = jnp.where(mine, part, total)
        return total

    dot = functools.partial(jnp.dot, preferred_element_type=jnp.float32)
    gram = lax.dot_general(
        stacked, stacked, (((1,), (1,)), ((), ())), preferred_element_type=jnp.float32
    )
    beside = gram[:row_count]
    for b in range(1, blocks):
        mine = lane // row_count == b
        beside = jnp.where(mine, gram[b * row_count : (b + 1) * row_count], beside)
    beside = beside * (1.0 / row_count)
    trace_sum = per_block(jnp.sum(beside * identity, axis=0, keepdims=True))
    squares = per_block(jnp.sum(beside * beside, axis=0, keepdims=True))
    damping = (DAMPING / order) * trace_sum
    frobenius = jnp.sqrt(squares + 2.0 * damping * trace_sum + order * damping * damping)
    scale = 1.0 / frobenius
    power = identity - (beside + damping * identity) * scale
    total = identity + power
    for step in range(NS_ITERS):
        high, low = halves(power)
        right_high, right_low = spread(high), spread(low)
        if step == 0:
            left_high, left_low = high.astype(jnp.bfloat16), low.astype(jnp.bfloat16)
        elif step < NS_ITERS - 1:
            total_high, total_low = halves(total)
            left_high = jnp.concatenate([total_high, high], axis=0).astype(jnp.bfloat16)
            left_low = jnp.concatenate([total_low, low], axis=0).astype(jnp.bfloat16)
        else:
            total_high, total_low = halves(total)
            left_high, left_low = total_high.astype(jnp.bfloat16), total_low.astype(jnp.bfloat16)
        product = dot(left_high, right_high) + (
            dot(left_high, right_low) + dot(left_low, right_high)
        )
        if step == 0:
            power = product
        else:
            total = total + product[:row_count]
            power = product[row_count:]
    high, low = halves(total * scale)
    return spread(high), spread(low)


def kernel(
    wide, lengths_hbm, act_ref, grad_ref, in_ref, out_proj_ref, result_ref,
    lengths_ref, act_v, grad_v, in_v, out_v, outgoing, rows_v, work, finished, returned,
    lengths_sem, load_sem, send_sem, recv_sem, back_send_sem, back_recv_sem,
):
    seqs, modules, seq_len, width = act_ref.shape
    rank_in = in_ref.shape[2]
    rank_out = out_proj_ref.shape[2]
    here = rank_out // wide
    all_seqs = seqs * wide
    lanes = BLOCK // rank_in
    blocks = here // lanes
    depth = width // CHUNKS
    me = lax.axis_index("wide")

    def loads(m, c):
        span = pl.ds(c * depth, depth)
        return (
            pltpu.make_async_copy(act_ref.at[:, m, :, span], act_v.at[m, c], load_sem.at[m, c, 0]),
            pltpu.make_async_copy(in_ref.at[m, span, :], in_v.at[m, c], load_sem.at[m, c, 1]),
            pltpu.make_async_copy(grad_ref.at[:, m, :, span], grad_v.at[m, c], load_sem.at[m, c, 2]),
            pltpu.make_async_copy(out_proj_ref.at[m, span, :], out_v.at[m, c], load_sem.at[m, c, 3]),
        )

    lengths_copy = pltpu.make_async_copy(lengths_hbm, lengths_ref, lengths_sem)
    lengths_copy.start()
    for c in range(CHUNKS):
        for copy in loads(0, c):
            copy.start()

    barrier = pltpu.get_barrier_semaphore()

    def greet(d, carry):
        pl.semaphore_signal(
            barrier, inc=1, device_id={"wide": lax.rem(me + d, wide)}, device_id_type=MESH
        )
        return carry

    lax.fori_loop(1, wide, greet, 0, unroll=5)

    def scatter(m, d):
        target = lax.rem(me + d, wide)
        return pltpu.make_async_remote_copy(
            src_ref=outgoing.at[m, target],
            dst_ref=rows_v.at[m, pl.ds(me * seqs, seqs)],
            send_sem=send_sem.at[m],
            recv_sem=recv_sem.at[m],
            device_id={"wide": target},
            device_id_type=MESH,
        )

    def give_back(m, d):
        target = lax.rem(me + d, wide)
        return pltpu.make_async_remote_copy(
            src_ref=finished.at[m, pl.ds(target * seqs, seqs)],
            dst_ref=returned.at[m, me],
            send_sem=back_send_sem.at[m],
            recv_sem=back_recv_sem.at[m, d],
            device_id={"wide": target},
            device_id_type=MESH,
        )

    def all_others(buffer, m, send, recv):
        part = buffer.at[m, pl.ds(0, (wide - 1) * seqs)]
        return pltpu.make_async_remote_copy(
            src_ref=part,
            dst_ref=part,
            send_sem=send,
            recv_sem=recv,
            device_id={"wide": lax.rem(me + 1, wide)},
            device_id_type=MESH,
        )

    def each(action):
        def body(i, carry):
            action(wide // 2 + (2 * (i % 2) - 1) * ((i + 1) // 2))
            return carry

        lax.fori_loop(0, wide - 1, body, 0, unroll=5)

    dot = functools.partial(jnp.dot, preferred_element_type=jnp.float32)
    positions = lax.broadcasted_iota(jnp.int32, (seq_len, 1), 0)
    for m in range(modules):
        acc_in = jnp.zeros((seqs * seq_len, rank_in), jnp.float32)
        acc_out = jnp.zeros((seqs * seq_len, rank_out), jnp.float32)
        for c in range(CHUNKS):
            for copy in loads(m, c):
                copy.wait()
            if m + 1 < modules:
                for copy in loads(m + 1, c):
                    copy.start()
            acc_in = acc_in + dot(act_v[m, c].reshape(seqs * seq_len, depth), in_v[m, c])
            acc_out = acc_out + dot(grad_v[m, c].reshape(seqs * seq_len, depth), out_v[m, c])
        if m == 0:
            lengths_copy.wait()
        for s in range(seqs):
            valid = jnp.where(positions < lengths_ref[s], 1.0, 0.0).astype(jnp.float32)
            part = slice(s * seq_len, (s + 1) * seq_len)
            left = (acc_out[part] * valid).astype(jnp.bfloat16)
            right = (acc_in[part] * valid).astype(jnp.bfloat16)
            product = lax.dot_general(
                left, right, (((0,), (0,)), ((), ())), preferred_element_type=jnp.float32
            ) * (1.0 / math.sqrt(seq_len))
            outgoing[m, :, s] = product.astype(jnp.bfloat16).reshape(wide, here, rank_in)
        if m == 0:
            pl.semaphore_wait(barrier, wide - 1)
        each(lambda d: scatter(m, d).start())
        rows_v[m, pl.ds(me * seqs, seqs)] = outgoing[m, me]

    def rounded(w):
        rows = seqs * here
        part = work[pl.ds(pl.multiple_of(w * rows, rows), rows), :]
        return part.astype(jnp.bfloat16).reshape(seqs, here, rank_in)

    masks = block_masks(blocks * all_seqs, all_seqs)
    for m in range(modules):
        all_others(rows_v, m, send_sem.at[m], recv_sem.at[m]).wait_recv()
        work[...] = rows_v[m].astype(jnp.float32).reshape(all_seqs * here, rank_in)
        stacked = jnp.concatenate(
            [
                jnp.concatenate(
                    [
                        work[pl.ds(b * lanes + j, all_seqs, stride=here), :].astype(jnp.bfloat16)
                        for j in range(lanes)
                    ],
                    axis=1,
                )
                for b in range(blocks)
            ],
            axis=0,
        )
        high, low = polynomial(stacked, BLOCK, all_seqs, masks)
        solved = dot(high, stacked) + dot(low, stacked)
        for b in range(blocks):
            for j in range(lanes):
                work[pl.ds(b * lanes + j, all_seqs, stride=here), :] = solved[
                    b * all_seqs : (b + 1) * all_seqs, j * rank_in : (j + 1) * rank_in
                ]

        def answer(d):
            finished[m, pl.ds(lax.rem(me + d, wide) * seqs, seqs)] = rounded(lax.rem(me + d, wide))
            give_back(m, d).start()

        each(answer)
        returned[m, me] = rounded(me)

    def place(m, w):
        rows = seqs * here
        top = pl.multiple_of(w * rows, rows)
        work[pl.ds(top, rows), :] = returned[m, w].astype(jnp.float32).reshape(rows, rank_in)
        for o in range(here):
            lane = pl.multiple_of(((m * wide + w) * here + o) * rank_in, rank_in)
            result_ref[:, pl.ds(lane, rank_in)] = work[
                pl.ds(top + o, seqs, stride=here), :
            ].astype(jnp.bfloat16)

    for m in range(modules):
        all_others(rows_v, m, send_sem.at[m], recv_sem.at[m]).wait_send()
        place(m, me)
    for m in range(modules):

        def take(i, carry):
            d = wide // 2 + (2 * (i % 2) - 1) * ((i + 1) // 2)
            give_back(m, d).wait_recv()
            place(m, lax.rem(me + wide - d, wide))
            return carry

        lax.fori_loop(0, wide - 1, take, 0)
    for m in range(modules):
        all_others(finished, m, back_send_sem.at[m], recv_sem.at[m]).wait_send()


def local_fused(wide, activations, out_grads, lengths, proj_in, proj_out):
    seqs, modules, seq_len, width = activations.shape
    rank_in = proj_in.shape[2]
    rank_out = proj_out.shape[2]
    here = rank_out // wide
    depth = width // CHUNKS
    all_seqs = seqs * wide
    hbm = pl.BlockSpec(memory_space=pltpu.HBM)
    bf16 = jnp.bfloat16
    return pl.pallas_call(
        functools.partial(kernel, wide),
        out_shape=pltpu.VMEM((seqs, modules * rank_out * rank_in), bf16),
        in_specs=[hbm] * 5,
        out_specs=pl.BlockSpec(memory_space=pltpu.VMEM),
        scratch_shapes=[
            pltpu.SMEM((seqs,), jnp.int32),
            pltpu.VMEM((modules, CHUNKS, seqs, seq_len, depth), bf16),
            pltpu.VMEM((modules, CHUNKS, seqs, seq_len, depth), bf16),
            pltpu.VMEM((modules, CHUNKS, depth, rank_in), bf16),
            pltpu.VMEM((modules, CHUNKS, depth, rank_out), bf16),
            pltpu.VMEM((modules, wide, seqs, here, rank_in), bf16),
            pltpu.VMEM((modules, all_seqs, here, rank_in), bf16),
            pltpu.VMEM((all_seqs * here, rank_in), jnp.float32),
            pltpu.VMEM((modules, all_seqs, here, rank_in), bf16),
            pltpu.VMEM((modules, wide, seqs, here, rank_in), bf16),
            pltpu.SemaphoreType.DMA,
            pltpu.SemaphoreType.DMA((modules, CHUNKS, 4)),
            pltpu.SemaphoreType.DMA((modules,)),
            pltpu.SemaphoreType.DMA((modules,)),
            pltpu.SemaphoreType.DMA((modules,)),
            pltpu.SemaphoreType.DMA((modules, wide)),
        ],
        compiler_params=pltpu.CompilerParams(
            collective_id=0, has_side_effects=True, vmem_limit_bytes=58 * 1024 * 1024
        ),
    )(lengths, activations, out_grads, proj_in, proj_out)


def solution(mesh):
    in_specs = (
        P(("grp", "wide"), None, None, None),
        P(("grp", "wide"), None, None, None),
        P(("grp", "wide")),
        P(),
        P(),
    )
    out_specs = P(("grp", "wide"), None)
    wide = mesh.shape["wide"]

    def local(activations, out_grads, lengths, proj_in, proj_out):
        here = proj_out.shape[2] // wide
        lanes = BLOCK // proj_in.shape[2]
        stacked = activations.shape[0] * wide * max(here // lanes, 1)
        if here % 16 == 0 and here % lanes == 0 and stacked <= 512:
            return local_fused(wide, activations, out_grads, lengths, proj_in, proj_out)
        return local_plain(activations, out_grads, lengths, proj_in, proj_out)

    return jax.shard_map(
        local, mesh=mesh, in_specs=in_specs, out_specs=out_specs, check_vma=False
    )
```

```python
import functools
import math

import jax
import jax.numpy as jnp
from jax import lax
from jax.experimental import pallas as pl
from jax.experimental.pallas import tpu as pltpu
from jax.sharding import PartitionSpec as P

BLOCK = 512
NS_ITERS = 5
DAMPING = 0.1
CHUNKS = 4
MESH = pl.DeviceIdType.MESH


def precondition(rows):
    row_count = rows.shape[0]
    order = rows.shape[2]
    highest = lax.Precision.HIGHEST
    identity = jnp.eye(row_count, dtype=jnp.float32)[None]
    gram = jnp.einsum("ska,tka->kst", rows, rows, preferred_element_type=jnp.float32) / row_count
    trace_sum = jnp.trace(gram, axis1=1, axis2=2)[:, None, None]
    damping = DAMPING * trace_sum / order
    squares = jnp.sum(gram * gram, axis=(1, 2), keepdims=True)
    frobenius = jnp.sqrt(squares + 2.0 * damping * trace_sum + order * damping * damping)
    power = identity - (gram + damping * identity) / frobenius
    total = identity + power
    for _ in range(NS_ITERS - 1):
        power = jnp.einsum("kab,kbc->kac", power, power, precision=highest)
        total = total + jnp.einsum("kab,kbc->kac", total, power, precision=highest)
    return jnp.einsum(
        "kst,tka->ska", total / frobenius, rows.astype(jnp.float32), precision=highest
    ).astype(jnp.bfloat16)


def local_plain(activations, out_grads, lengths, proj_in, proj_out):
    seq_count, module_count, seq_len, model_width = activations.shape
    rank_in = proj_in.shape[2]
    rank_out = proj_out.shape[2]
    acc_in = jnp.einsum("smtd,mdr->smtr", activations, proj_in, preferred_element_type=jnp.float32)
    acc_out = jnp.einsum("smtd,mdr->smtr", out_grads, proj_out, preferred_element_type=jnp.float32)
    positions = lax.broadcasted_iota(jnp.int32, (seq_count, seq_len), 1)
    valid_mask = (positions < lengths[:, None]).astype(jnp.float32)[:, None, :, None]
    projected_in = (acc_in * valid_mask).astype(jnp.bfloat16)
    projected_out = (acc_out * valid_mask).astype(jnp.bfloat16)
    seq_grads = jnp.einsum(
        "smto,smti->smoi", projected_out, projected_in, preferred_element_type=jnp.float32
    ) * (1.0 / math.sqrt(seq_len))
    grad_size = module_count * rank_out * rank_in
    wide_count = lax.axis_size("wide")
    blocks_here = grad_size // (BLOCK * wide_count)
    blocks = seq_grads.astype(jnp.bfloat16).reshape(seq_count, wide_count, blocks_here, BLOCK)
    owned_rows = lax.all_to_all(blocks, "wide", split_axis=1, concat_axis=0, tiled=True)
    result = precondition(owned_rows[:, 0])[:, None]
    returned = lax.all_to_all(result, "wide", split_axis=0, concat_axis=1, tiled=True)
    return returned.reshape(seq_count, grad_size)


def block_masks(size, row_count):
    row = lax.broadcasted_iota(jnp.int32, (size, size), 0)
    column = lax.broadcasted_iota(jnp.int32, (size, size), 1)
    mask = jnp.where(row // row_count == column // row_count, 1.0, 0.0).astype(jnp.bfloat16)
    short = (row_count, size)
    on_diagonal = (
        lax.broadcasted_iota(jnp.int32, short, 0)
        == lax.broadcasted_iota(jnp.int32, short, 1) % row_count
    )
    return mask, jnp.where(on_diagonal, 1.0, 0.0).astype(jnp.float32)


def polynomial(stacked, order, row_count, masks):
    size = stacked.shape[0]
    blocks = size // row_count
    mask, identity = masks
    lane = lax.broadcasted_iota(jnp.int32, (1, size), 1)

    def spread(beside):
        return jnp.concatenate([beside.astype(jnp.bfloat16)] * blocks, axis=0) * mask

    def halves(beside):
        high = beside.astype(jnp.bfloat16).astype(jnp.float32)
        return high, beside - high

    def per_block(values):
        total = jnp.zeros((1, size), jnp.float32)
        for b in range(blocks):
            mine = lane // row_count == b
            part = jnp.sum(jnp.where(mine, values, 0.0), axis=1, keepdims=True)
            total = jnp.where(mine, part, total)
        return total

    dot = functools.partial(jnp.dot, preferred_element_type=jnp.float32)
    gram = lax.dot_general(
        stacked, stacked, (((1,), (1,)), ((), ())), preferred_element_type=jnp.float32
    )
    beside = gram[:row_count]
    for b in range(1, blocks):
        mine = lane // row_count == b
        beside = jnp.where(mine, gram[b * row_count : (b + 1) * row_count], beside)
    beside = beside * (1.0 / row_count)
    trace_sum = per_block(jnp.sum(beside * identity, axis=0, keepdims=True))
    squares = per_block(jnp.sum(beside * beside, axis=0, keepdims=True))
    damping = (DAMPING / order) * trace_sum
    frobenius = jnp.sqrt(squares + 2.0 * damping * trace_sum + order * damping * damping)
    scale = 1.0 / frobenius
    power = identity - (beside + damping * identity) * scale
    total = identity + power
    for step in range(NS_ITERS):
        high, low = halves(power)
        right_high, right_low = spread(high), spread(low)
        if step == 0:
            left_high, left_low = high.astype(jnp.bfloat16), low.astype(jnp.bfloat16)
        elif step < NS_ITERS - 1:
            total_high, total_low = halves(total)
            left_high = jnp.concatenate([total_high, high], axis=0).astype(jnp.bfloat16)
            left_low = jnp.concatenate([total_low, low], axis=0).astype(jnp.bfloat16)
        else:
            total_high, total_low = halves(total)
            left_high, left_low = total_high.astype(jnp.bfloat16), total_low.astype(jnp.bfloat16)
        product = dot(left_high, right_high) + (
            dot(left_high, right_low) + dot(left_low, right_high)
        )
        if step == 0:
            power = product
        else:
            total = total + product[:row_count]
            power = product[row_count:]
    high, low = halves(total * scale)
    return spread(high), spread(low)


def kernel(
    wide, lengths_hbm, act_ref, grad_ref, in_ref, out_proj_ref, result_ref,
    lengths_ref, act_v, grad_v, in_v, out_v, outgoing, rows_v, work, finished, returned,
    lengths_sem, load_sem, send_sem, recv_sem, back_send_sem, back_recv_sem,
):
    seqs, modules, seq_len, width = act_ref.shape
    rank_in = in_ref.shape[2]
    rank_out = out_proj_ref.shape[2]
    here = rank_out // wide
    all_seqs = seqs * wide
    lanes = BLOCK // rank_in
    blocks = here // lanes
    depth = width // CHUNKS
    me = lax.axis_index("wide")

    def loads(m, c):
        span = pl.ds(c * depth, depth)
        return (
            pltpu.make_async_copy(act_ref.at[:, m, :, span], act_v.at[m, c], load_sem.at[m, c, 0]),
            pltpu.make_async_copy(in_ref.at[m, span, :], in_v.at[m, c], load_sem.at[m, c, 1]),
            pltpu.make_async_copy(grad_ref.at[:, m, :, span], grad_v.at[m, c], load_sem.at[m, c, 2]),
            pltpu.make_async_copy(out_proj_ref.at[m, span, :], out_v.at[m, c], load_sem.at[m, c, 3]),
        )

    lengths_copy = pltpu.make_async_copy(lengths_hbm, lengths_ref, lengths_sem)
    lengths_copy.start()
    for c in range(CHUNKS):
        for copy in loads(0, c):
            copy.start()

    barrier = pltpu.get_barrier_semaphore()

    def greet(d, carry):
        pl.semaphore_signal(
            barrier, inc=1, device_id={"wide": lax.rem(me + d, wide)}, device_id_type=MESH
        )
        return carry

    lax.fori_loop(1, wide, greet, 0, unroll=5)

    def scatter(m, d):
        target = lax.rem(me + d, wide)
        return pltpu.make_async_remote_copy(
            src_ref=outgoing.at[m, target],
            dst_ref=rows_v.at[m, pl.ds(me * seqs, seqs)],
            send_sem=send_sem.at[m],
            recv_sem=recv_sem.at[m],
            device_id={"wide": target},
            device_id_type=MESH,
        )

    def give_back(m, d):
        target = lax.rem(me + d, wide)
        return pltpu.make_async_remote_copy(
            src_ref=finished.at[m, pl.ds(target * seqs, seqs)],
            dst_ref=returned.at[m, me],
            send_sem=back_send_sem.at[m],
            recv_sem=back_recv_sem.at[m, d],
            device_id={"wide": target},
            device_id_type=MESH,
        )

    def all_others(buffer, m, send, recv):
        part = buffer.at[m, pl.ds(0, (wide - 1) * seqs)]
        return pltpu.make_async_remote_copy(
            src_ref=part,
            dst_ref=part,
            send_sem=send,
            recv_sem=recv,
            device_id={"wide": lax.rem(me + 1, wide)},
            device_id_type=MESH,
        )

    def each(action):
        def body(i, carry):
            action(lax.rem((i + 1) * (wide // 2 - 1), wide))
            return carry

        lax.fori_loop(0, wide - 1, body, 0, unroll=5)

    dot = functools.partial(jnp.dot, preferred_element_type=jnp.float32)
    positions = lax.broadcasted_iota(jnp.int32, (seq_len, 1), 0)
    for m in range(modules):
        acc_in = jnp.zeros((seqs * seq_len, rank_in), jnp.float32)
        acc_out = jnp.zeros((seqs * seq_len, rank_out), jnp.float32)
        for c in range(CHUNKS):
            for copy in loads(m, c):
                copy.wait()
            if m + 1 < modules:
                for copy in loads(m + 1, c):
                    copy.start()
            acc_in = acc_in + dot(act_v[m, c].reshape(seqs * seq_len, depth), in_v[m, c])
            acc_out = acc_out + dot(grad_v[m, c].reshape(seqs * seq_len, depth), out_v[m, c])
        if m == 0:
            lengths_copy.wait()
        for s in range(seqs):
            valid = jnp.where(positions < lengths_ref[s], 1.0, 0.0).astype(jnp.float32)
            part = slice(s * seq_len, (s + 1) * seq_len)
            left = (acc_out[part] * valid).astype(jnp.bfloat16)
            right = (acc_in[part] * valid).astype(jnp.bfloat16)
            product = lax.dot_general(
                left, right, (((0,), (0,)), ((), ())), preferred_element_type=jnp.float32
            ) * (1.0 / math.sqrt(seq_len))
            outgoing[m, :, s] = product.astype(jnp.bfloat16).reshape(wide, here, rank_in)
        if m == 0:
            pl.semaphore_wait(barrier, wide - 1)
        each(lambda d: scatter(m, d).start())
        rows_v[m, pl.ds(me * seqs, seqs)] = outgoing[m, me]

    def rounded(w):
        rows = seqs * here
        part = work[pl.ds(pl.multiple_of(w * rows, rows), rows), :]
        return part.astype(jnp.bfloat16).reshape(seqs, here, rank_in)

    masks = block_masks(blocks * all_seqs, all_seqs)
    for m in range(modules):
        all_others(rows_v, m, send_sem.at[m], recv_sem.at[m]).wait_recv()
        work[...] = rows_v[m].astype(jnp.float32).reshape(all_seqs * here, rank_in)
        stacked = jnp.concatenate(
            [
                jnp.concatenate(
                    [
                        work[pl.ds(b * lanes + j, all_seqs, stride=here), :].astype(jnp.bfloat16)
                        for j in range(lanes)
                    ],
                    axis=1,
                )
                for b in range(blocks)
            ],
            axis=0,
        )
        high, low = polynomial(stacked, BLOCK, all_seqs, masks)
        solved = dot(high, stacked) + dot(low, stacked)
        for b in range(blocks):
            for j in range(lanes):
                work[pl.ds(b * lanes + j, all_seqs, stride=here), :] = solved[
                    b * all_seqs : (b + 1) * all_seqs, j * rank_in : (j + 1) * rank_in
                ]

        def answer(d):
            finished[m, pl.ds(lax.rem(me + d, wide) * seqs, seqs)] = rounded(lax.rem(me + d, wide))
            give_back(m, d).start()

        each(answer)
        returned[m, me] = rounded(me)

    def place(m, w):
        rows = seqs * here
        top = pl.multiple_of(w * rows, rows)
        work[pl.ds(top, rows), :] = returned[m, w].astype(jnp.float32).reshape(rows, rank_in)
        for o in range(here):
            lane = pl.multiple_of(((m * wide + w) * here + o) * rank_in, rank_in)
            result_ref[:, pl.ds(lane, rank_in)] = work[
                pl.ds(top + o, seqs, stride=here), :
            ].astype(jnp.bfloat16)

    for m in range(modules):
        all_others(rows_v, m, send_sem.at[m], recv_sem.at[m]).wait_send()
        place(m, me)
    for m in range(modules):

        def take(i, carry):
            d = lax.rem((i + 1) * (wide // 2 - 1), wide)
            give_back(m, d).wait_recv()
            place(m, lax.rem(me + wide - d, wide))
            return carry

        lax.fori_loop(0, wide - 1, take, 0)
    for m in range(modules):
        all_others(finished, m, back_send_sem.at[m], recv_sem.at[m]).wait_send()


def local_fused(wide, activations, out_grads, lengths, proj_in, proj_out):
    seqs, modules, seq_len, width = activations.shape
    rank_in = proj_in.shape[2]
    rank_out = proj_out.shape[2]
    here = rank_out // wide
    depth = width // CHUNKS
    all_seqs = seqs * wide
    hbm = pl.BlockSpec(memory_space=pltpu.HBM)
    bf16 = jnp.bfloat16
    return pl.pallas_call(
        functools.partial(kernel, wide),
        out_shape=pltpu.VMEM((seqs, modules * rank_out * rank_in), bf16),
        in_specs=[hbm] * 5,
        out_specs=pl.BlockSpec(memory_space=pltpu.VMEM),
        scratch_shapes=[
            pltpu.SMEM((seqs,), jnp.int32),
            pltpu.VMEM((modules, CHUNKS, seqs, seq_len, depth), bf16),
            pltpu.VMEM((modules, CHUNKS, seqs, seq_len, depth), bf16),
            pltpu.VMEM((modules, CHUNKS, depth, rank_in), bf16),
            pltpu.VMEM((modules, CHUNKS, depth, rank_out), bf16),
            pltpu.VMEM((modules, wide, seqs, here, rank_in), bf16),
            pltpu.VMEM((modules, all_seqs, here, rank_in), bf16),
            pltpu.VMEM((all_seqs * here, rank_in), jnp.float32),
            pltpu.VMEM((modules, all_seqs, here, rank_in), bf16),
            pltpu.VMEM((modules, wide, seqs, here, rank_in), bf16),
            pltpu.SemaphoreType.DMA,
            pltpu.SemaphoreType.DMA((modules, CHUNKS, 4)),
            pltpu.SemaphoreType.DMA((modules,)),
            pltpu.SemaphoreType.DMA((modules,)),
            pltpu.SemaphoreType.DMA((modules,)),
            pltpu.SemaphoreType.DMA((modules, wide)),
        ],
        compiler_params=pltpu.CompilerParams(
            collective_id=0, has_side_effects=True, vmem_limit_bytes=58 * 1024 * 1024
        ),
    )(lengths, activations, out_grads, proj_in, proj_out)


def solution(mesh):
    in_specs = (
        P(("grp", "wide"), None, None, None),
        P(("grp", "wide"), None, None, None),
        P(("grp", "wide")),
        P(),
        P(),
    )
    out_specs = P(("grp", "wide"), None)
    wide = mesh.shape["wide"]

    def local(activations, out_grads, lengths, proj_in, proj_out):
        here = proj_out.shape[2] // wide
        lanes = BLOCK // proj_in.shape[2]
        stacked = activations.shape[0] * wide * max(here // lanes, 1)
        if wide % 4 == 0 and here % 16 == 0 and here % lanes == 0 and stacked <= 512:
            return local_fused(wide, activations, out_grads, lengths, proj_in, proj_out)
        return local_plain(activations, out_grads, lengths, proj_in, proj_out)

    return jax.shard_map(
        local, mesh=mesh, in_specs=in_specs, out_specs=out_specs, check_vma=False
    )
```
